512 devices in a mesh: ctx: 32 (over y, x), head: 16 (over z, core).
Axes of the slice: x: 4, y: 8, z: 8, core: 2. Of those that a mesh axis runs over, the one named last changes fastest.
Arguments:
- latent: bfloat16 [40960, 576], P('ctx'), may hold values from -7 to 7
- query: bfloat16 [4096, 36864], P('ctx', 'head'), may hold values from -200 to 200
- grad_out: bfloat16 [4096, 32768], P('ctx', 'head'), may hold values from -6 to 6
- picks: int32 [4096, 32], P('ctx'), may hold values from 0 to 639, as said below
Outputs:
- grad_query: bfloat16 [4096, 36864], P('ctx', 'head')
- grad_latent: float32 [40960, 576], P(('ctx', 'head'))
The draws below stay inside these ranges and needn't reach their ends.
Inputs may be any that keep to these rules, and one draw needn't show every extreme that they name: `picks`: the 32 blocks of a query are distinct, none past the block of the last query held by the same index of ctx; blocks past a query's own position are padding. The queries of one index of ctx pick exactly 36 distinct blocks together, always including the blocks that hold those queries, and at most 2 of them lie on one index of ctx; every device's pool reaches that bound on some index.
All inputs are finite; a program needn't handle non-finite values.
Results may differ from the reference program's by a relative error of at most 0.0049.
Values may be sent and summed in bfloat16 or wider, within the bound.
No kernel may reach another device: no remote copies, remote signals or barrier semaphores. Data moves between devices by JAX's collectives and lax.ppermute only.
A program may use at most 128 MiB of HBM per device.

```python
import math
import jax
import jax.numpy as jnp
from jax import lax

HEADS = 64
LAT = 512
ROPE = 64
KW = 576
BLOCK = 64
PICKS = 32
POOL = 36
Q_DEV = 128
CTX_DEV = 1280
QUERIES = 4096
CONTEXT = 40960
CAP = 2
N_CTX = 32


def pick_lists(key):
    base = jax.random.fold_in(key, 101)
    nblocks = CONTEXT // BLOCK
    per_owner = CTX_DEV // BLOCK
    first_token = CONTEXT - QUERIES
    block_ids = jnp.arange(nblocks, dtype=jnp.int32)
    owners = block_ids // per_owner

    def one_shard(shard_id, shard_key):
        first_block = (first_token + shard_id * Q_DEV) // BLOCK
        last_block = (first_token + (shard_id + 1) * Q_DEV - 1) // BLOCK
        noise_key, order_key = jax.random.split(shard_key)
        noise = jax.random.randint(noise_key, (nblocks,), 0, 2048, dtype=jnp.int32)
        scores = (noise + block_ids * 2048 // nblocks) * nblocks + block_ids
        usable = block_ids <= last_block
        own = usable & (block_ids >= first_block)
        boosted = scores + own.astype(jnp.int32) * 67108864
        grid = jnp.where(usable, boosted, -1 - block_ids).reshape(N_CTX, per_owner)
        ranks = jnp.sum(grid[:, None, :] > grid[:, :, None], axis=2).reshape(nblocks)
        eligible = usable & (ranks < CAP)
        favoured = eligible & (owners == first_block // per_owner - 1)
        final = jnp.where(eligible, boosted + favoured.astype(jnp.int32) * 67108864, -1 - block_ids)
        pool = jnp.sort(lax.top_k(final, POOL)[1]).astype(jnp.int32)
        forced = jnp.arange(Q_DEV, dtype=jnp.int32) % POOL
        shuffles = jax.vmap(lambda row_key: jax.random.permutation(row_key, POOL - 1))(jax.random.split(order_key, Q_DEV))
        others = (forced[:, None] + 1 + shuffles[:, :PICKS - 1].astype(jnp.int32)) % POOL
        slots = jnp.concatenate([forced[:, None], others], axis=1)
        return (pool, pool[slots])
    pools, lists = jax.vmap(one_shard)(jnp.arange(N_CTX, dtype=jnp.int32), jax.random.split(base, N_CTX))
    return lists.reshape(QUERIES, PICKS)


def latent_rows(key):
    base = jax.random.fold_in(key, 202)
    normal_key = jax.random.fold_in(base, 0)
    gauss = jnp.clip(jax.random.normal(normal_key, (CONTEXT, LAT + ROPE), jnp.float32), -4.0, 4.0)
    return gauss


def draw_latent(key, part):
    rows = latent_rows(key)
    return rows.astype(jnp.bfloat16)


def draw_query(key, part):
    own_key = jax.random.fold_in(key, 2)
    values = jnp.clip(jax.random.normal(own_key, (QUERIES, HEADS, LAT + ROPE), jnp.float32), -4.0, 4.0)
    return values.reshape(QUERIES, HEADS * (LAT + ROPE)).astype(jnp.bfloat16)


def draw_picks(key, part):
    lists = pick_lists(key)
    return lists


def block_scale(rng, dims, shards, low, largest):
    loudness = 1.0
    for axis_at, blocks in shards:
        heights = jax.random.uniform(jax.random.fold_in(jax.random.fold_in(rng, 6), axis_at), (blocks,), jnp.float32, low / len(shards), largest / len(shards))
        loudness = loudness * jnp.repeat(jnp.exp(heights), dims[axis_at] // blocks).reshape((-1,) + (1,) * (len(dims) - 1 - axis_at))
    return loudness


def bell_draw(stream_key, extent, width, most, pieces=(), held_as=jnp.bfloat16):
    result = width * jax.random.normal(stream_key, extent, jnp.float32)
    if pieces:
        result = result * block_scale(stream_key, extent, pieces, -0.22, 0.18)
    return jnp.clip(result, -most, most).astype(held_as)


def setup_inputs(seed: int = 0) -> dict:
    key_of = jax.random.split(jax.random.key(seed), 5)
    latent = draw_latent(jax.random.fold_in(key_of[4], 71), 0)
    query = draw_query(jax.random.fold_in(key_of[4], 71), 0)
    grad_out = bell_draw(key_of[2], (QUERIES, HEADS * LAT), 1.0, 6.0, ((0, 32), (1, 16)))
    picks = draw_picks(jax.random.fold_in(key_of[4], 71), 0)
    return {"latent": latent, "query": query, "grad_out": grad_out, "picks": picks}


score_scale = 192.0 ** -0.5


def one_batch(latent, query_batch, grad_batch, pick_batch, query_pos):
    offsets = jnp.arange(BLOCK, dtype=jnp.int32)

    def single(query_row, grad_row, pick_row, position):
        tokens = (pick_row[:, None] * BLOCK + offsets[None, :]).reshape(-1).astype(jnp.int32)
        key_rows = latent[tokens]
        scores = jnp.dot(query_row, key_rows.T, preferred_element_type=jnp.float32) * score_scale
        masked = jnp.where((tokens <= position)[None, :], scores, -jnp.inf)
        row_max = jnp.max(masked, axis=1, keepdims=True)
        exponent = jnp.exp(masked - row_max)
        attn_probs = exponent / jnp.sum(exponent, axis=1, keepdims=True)
        probs_low = attn_probs.astype(jnp.bfloat16)
        prob_grad = jnp.dot(grad_row, key_rows[:, :LAT].T, preferred_element_type=jnp.float32)
        row_delta = jnp.sum(attn_probs * prob_grad, axis=1, keepdims=True)
        dscore = (attn_probs * (prob_grad - row_delta)).astype(jnp.bfloat16)
        query_grad = (jnp.dot(dscore, key_rows, preferred_element_type=jnp.float32) * score_scale).astype(jnp.bfloat16)
        key_grad = jnp.dot(dscore.T, query_row, preferred_element_type=jnp.float32) * score_scale
        value_grad = jnp.dot(probs_low.T, grad_row, preferred_element_type=jnp.float32)
        key_grad = jnp.concatenate([key_grad[:, :LAT] + value_grad, key_grad[:, LAT:]], axis=1)
        return query_grad, key_grad, tokens

    return jax.vmap(single)(query_batch, grad_batch, pick_batch, query_pos)


def reference(latent, query, grad_out, picks):
    batch = math.gcd(QUERIES, 16)
    step_count = QUERIES // batch
    query_heads = query.reshape(step_count, batch, HEADS, KW)
    grad_heads = grad_out.reshape(step_count, batch, HEADS, LAT)
    pick_groups = picks.reshape(step_count, batch, PICKS)
    positions = (CONTEXT - QUERIES + jnp.arange(QUERIES, dtype=jnp.int32)).reshape(step_count, batch)

    def step(carry, item):
        query_batch, grad_batch, pick_batch, query_pos = item
        query_grad, key_grad, tokens = one_batch(latent, query_batch, grad_batch, pick_batch, query_pos)
        carry = carry.at[tokens.reshape(-1)].add(key_grad.reshape(-1, KW))
        return carry, query_grad

    grad_latent, query_grads = lax.scan(step, jnp.zeros((CONTEXT, KW), jnp.float32), (query_heads, grad_heads, pick_groups, positions))
    return query_grads.reshape(QUERIES, HEADS * KW), grad_latent
```

```python
import functools

import jax
import jax.numpy as jnp
from jax import lax
from jax.experimental import pallas as pl
from jax.experimental.pallas import tpu as pltpu
from jax.sharding import PartitionSpec as P

LAT = 512
BLOCK = 64
POOL = 36
CAP = 2
NEG = -1e30

score_scale = 192.0 ** (-0.5)
bf16 = jnp.bfloat16
f32 = jnp.float32


def iota(shape, dim):
    return lax.broadcasted_iota(jnp.int32, shape, dim)


def by20(x):
    return (x * 3277) >> 16


def dot(a, b, ca, cb):
    return lax.dot_general(a, b, (((ca,), (cb,)), ((), ())), preferred_element_type=f32)


def call(body, out_shape, *args, scratch=(), flops=0, traffic=0):
    vmem = pl.BlockSpec(memory_space=pltpu.VMEM)
    smem = pl.BlockSpec(memory_space=pltpu.SMEM)
    specs = [smem if a.dtype == jnp.int32 and a.ndim == 1 else vmem for a in args]
    return pl.pallas_call(
        body,
        out_shape=out_shape,
        in_specs=specs,
        out_specs=jax.tree.map(lambda _: vmem, out_shape),
        scratch_shapes=list(scratch),
        compiler_params=pltpu.CompilerParams(vmem_limit_bytes=48 * 1024 * 1024),
        cost_estimate=pl.CostEstimate(flops=flops, bytes_accessed=traffic, transcendentals=0),
    )(*args)


def own_rows(pos_ref, lat_ref, out_ref, *, part):
    rows, tokens = out_ref.shape[0], lat_ref.shape[0]
    row, col = iota((rows, tokens), 0), iota((rows, tokens), 1)
    want = (row >> 2) * BLOCK + pos_ref[1] * part + (row & 3)
    pick = (col == want).astype(f32).astype(bf16)
    out_ref[...] = dot(pick, lat_ref[...], 1, 0).astype(bf16)


def plan(pos_ref, picks_ref, sel_ref, bias_ref, send_ref, local_ref, *, part, per_owner, first):
    queries, picks = picks_ref.shape
    rows, wide = sel_ref.shape
    blocks = wide // part
    parts = BLOCK // part
    lane = iota((queries, blocks), 1)
    hit = jnp.zeros((queries, blocks), jnp.bool_)
    for k in range(picks):
        hit = jnp.logical_or(hit, picks_ref[:, k : k + 1] == lane)
    hit = hit.astype(f32)
    chosen = jnp.max(hit, axis=0, keepdims=True)
    hit = hit.astype(bf16)
    chosen8 = jnp.broadcast_to(chosen, (8, blocks)).astype(bf16)
    lo, hi = iota((blocks, blocks), 0), iota((blocks, blocks), 1)
    before = jnp.where(lo < hi, 1.0, 0.0)
    order = dot(chosen8, before.astype(bf16), 1, 0)[:1]
    same = jnp.where(by20(lo) == by20(hi), before, 0.0)
    rank = dot(chosen8, same.astype(bf16), 1, 0)[:1]
    row = iota((rows, blocks), 0)
    slot = ((row >> 2)).astype(f32)
    here = jnp.where(jnp.logical_and(order == slot, chosen > 0.5), 1.0, 0.0)
    block_id = jnp.sum(here * iota((rows, blocks), 1).astype(f32), axis=1, keepdims=True)
    block_rank = jnp.sum(here * rank, axis=1, keepdims=True)
    block_id = block_id.astype(jnp.int32)
    block_rank = block_rank.astype(jnp.int32)
    row = iota((rows, wide), 0)
    col = iota((rows, wide), 1)
    sel = col == block_id * part + (row & 3)
    sel_ref[...] = jnp.where(sel, 1.0, 0.0).astype(bf16)
    picked = dot(here.astype(bf16), hit, 1, 1)
    query_pos = first + pos_ref[0] * queries + iota((rows, queries), 1)
    for p in range(parts):
        key_pos = block_id * BLOCK + p * part + (iota((rows, queries), 0) & 3)
        allowed = jnp.logical_and(picked > 0.5, key_pos <= query_pos)
        bias_ref[p * rows : (p + 1) * rows, :] = jnp.where(allowed, 0.0, NEG)
    owner = by20(block_id)
    local_id = block_id - owner * per_owner
    row = iota(send_ref.shape, 0)
    col = iota(send_ref.shape, 1)
    target = (owner * CAP + block_rank) * part + (row & 3)
    send_ref[...] = jnp.where(col == target, 1.0, 0.0).astype(bf16)
    lane = iota(local_ref.shape, 1)
    local_ref[...] = jnp.where(lane == 0, local_id.astype(f32), jnp.where(lane == 1, 1.0, 0.0))


def compact(sel_ref, all_ref, out_ref):
    out_ref[...] = dot(sel_ref[...], all_ref[...], 1, 0).astype(bf16)


def attend(k_ref, q_ref, g_ref, bias_ref, dq_ref, dk_ref, s_ref, d_ref, qs_ref, gs_ref, dqs_ref):
    tokens, width = k_ref.shape
    queries = q_ref.shape[0]
    heads = g_ref.shape[1] // LAT
    cols = heads * queries
    step = 256
    steps = tokens // step
    for h in range(heads):
        qs_ref[h * queries : (h + 1) * queries, :] = q_ref[:, h * width : (h + 1) * width]
        gs_ref[h * queries : (h + 1) * queries, :] = g_ref[:, h * LAT : (h + 1) * LAT]

    def one(i, top):
        at = pl.ds(pl.multiple_of(i * step, step), step)
        keys = k_ref[at, :]
        bias = bias_ref[at, :]
        s = dot(keys, qs_ref[...], 1, 1) * score_scale + jnp.concatenate([bias] * heads, axis=1)
        s_ref[at, :] = s
        d_ref[at, :] = dot(keys[:, :LAT], gs_ref[...], 1, 1)
        return jnp.maximum(top, jnp.max(s.reshape(step // 8, 8, cols), axis=0))

    top = lax.fori_loop(0, steps, one, jnp.full((8, cols), -jnp.inf, f32))
    top = jnp.max(top, axis=0, keepdims=True)

    def two(i, carry):
        total, mixed = carry
        at = pl.ds(pl.multiple_of(i * step, step), step)
        e = jnp.exp(s_ref[at, :] - top)
        s_ref[at, :] = e
        ed = e * d_ref[at, :]
        total = total + jnp.sum(e.reshape(step // 8, 8, cols), axis=0)
        mixed = mixed + jnp.sum(ed.reshape(step // 8, 8, cols), axis=0)
        return total, mixed

    zero = jnp.zeros((8, cols), f32)
    total, mixed = lax.fori_loop(0, steps, two, (zero, zero))
    inv = 1.0 / jnp.sum(total, axis=0, keepdims=True)
    delta = jnp.sum(mixed, axis=0, keepdims=True) * inv
    dqs_ref[...] = jnp.zeros_like(dqs_ref)

    def three(i, carry):
        at = pl.ds(pl.multiple_of(i * step, step), step)
        p = s_ref[at, :] * inv
        ds = (p * (d_ref[at, :] - delta)).astype(bf16)
        dk = dot(ds, qs_ref[...], 1, 0) * score_scale
        dv = dot(p.astype(bf16), gs_ref[...], 1, 0)
        dk_ref[at, :LAT] = (dk[:, :LAT] + dv).astype(dk_ref.dtype)
        dk_ref[at, LAT:] = dk[:, LAT:].astype(dk_ref.dtype)
        dqs_ref[...] += dot(ds, k_ref[at, :], 0, 0)
        return carry

    lax.fori_loop(0, steps, three, 0)
    for h in range(heads):
        part = dqs_ref[h * queries : (h + 1) * queries, :] * score_scale
        dq_ref[:, h * width : (h + 1) * width] = part.astype(bf16)


def outgoing(send_ref, grad_ref, local_ref, out_ref):
    width = grad_ref.shape[1]
    send = send_ref[...]
    out_ref[:, :LAT] = dot(send, grad_ref[:, :LAT].astype(bf16), 0, 0).astype(bf16)
    tail = jnp.concatenate(
        [grad_ref[:, LAT:].astype(f32), local_ref[:, : 128 - (width - LAT)]], axis=1
    ).astype(bf16)
    out_ref[:, LAT:] = dot(send, tail, 0, 0).astype(bf16)


def gather_back(pos_ref, in_ref, out_ref, *, part, width):
    rows = in_ref.shape[0]
    outs = out_ref.shape[0]
    parts = BLOCK // part
    mine = pos_ref[1]
    ids = in_ref[:, LAT:].astype(f32)
    lane = iota(ids.shape, 1)
    block = jnp.sum(jnp.where(lane == width - LAT, ids, 0.0), axis=1, keepdims=True)
    valid = jnp.sum(jnp.where(lane == width - LAT + 1, ids, 0.0), axis=1, keepdims=True)
    block = block.astype(jnp.int32)
    row = iota((rows, outs), 0)
    col = iota((rows, outs), 1)
    chunks = outs // part
    per_dest = 20
    dest = col >> 3
    which = (col >> 2) & 1
    start = ((per_dest * dest - mine + parts - 1) >> 4) + which
    inside = parts * start + mine < per_dest * (dest + 1)
    match = jnp.logical_and(block == start, (row & 3) == (col & 3))
    match = jnp.logical_and(match, jnp.logical_and(inside, valid > 0.5))
    out_ref[...] = dot(jnp.where(match, 1.0, 0.0).astype(bf16), in_ref[:, :width], 0, 0)


def place(pos_ref, in_ref, out_ref, *, part):
    outs = out_ref.shape[0]
    rows = in_ref.shape[0]
    parts = BLOCK // part
    per_dest = outs // part
    mine = pos_ref[1]
    row = iota((outs, rows), 0)
    col = iota((outs, rows), 1)
    chunk = per_dest * mine + (row >> 2)
    source = col >> 3
    which = (col >> 2) & 1
    start = ((per_dest * mine - source + parts - 1) >> 4) + which
    match = jnp.logical_and(parts * start + source == chunk, (row & 3) == (col & 3))
    out_ref[...] = lax.dot_general(
        jnp.where(match, 1.0, 0.0),
        in_ref[...].astype(f32),
        (((1,), (0,)), ((), ())),
        precision=lax.Precision.HIGHEST,
        preferred_element_type=f32,
    )


def local(latent, query, grad_out, picks):
    n_ctx = lax.axis_size("ctx")
    n_head = lax.axis_size("head")
    ctx_rows, width = latent.shape
    queries = query.shape[0]
    per_owner = ctx_rows // BLOCK
    blocks = per_owner * n_ctx
    part = BLOCK // n_head
    pool_rows = POOL * part
    pos = jnp.stack([lax.axis_index("ctx"), lax.axis_index("head")]).astype(jnp.int32)
    first = (ctx_rows - queries) * n_ctx
    shape = jax.ShapeDtypeStruct

    own = call(
        functools.partial(own_rows, part=part),
        shape((per_owner * part, width), bf16),
        pos,
        latent,
    )
    everyone = lax.all_gather(own, "ctx", axis=0, tiled=True)
    sel, bias, send, local_id = call(
        functools.partial(plan, part=part, per_owner=per_owner, first=first),
        (
            shape((pool_rows, blocks * part), bf16),
            shape((POOL * BLOCK, queries), f32),
            shape((pool_rows, n_ctx * CAP * part), bf16),
            shape((pool_rows, 128), f32),
        ),
        pos,
        picks,
        flops=4 * 10**9,
        traffic=4 * 10**6,
    )
    mine = call(compact, shape((pool_rows, width), bf16), sel, everyone)
    keys = lax.all_gather(mine, "head", axis=0, tiled=True)
    tokens = POOL * BLOCK
    rows = queries * (grad_out.shape[1] // LAT)
    query_grad, key_grad = call(
        attend,
        (shape(query.shape, bf16), shape((tokens, width), f32)),
        keys,
        query,
        grad_out,
        bias,
        scratch=(
            pltpu.VMEM((tokens, rows), f32),
            pltpu.VMEM((tokens, rows), f32),
            pltpu.VMEM((rows, width), bf16),
            pltpu.VMEM((rows, LAT), bf16),
            pltpu.VMEM((rows, width), f32),
        ),
        flops=7 * 10**9,
        traffic=10**7,
    )
    reduced = lax.psum_scatter(key_grad, "head", scatter_dimension=0, tiled=True)
    slots = n_ctx * CAP * part
    outbox = call(outgoing, shape((slots, 640), bf16), send, reduced, local_id)
    inbox = lax.all_to_all(outbox, "ctx", split_axis=0, concat_axis=0, tiled=True)
    totals = call(
        functools.partial(gather_back, part=part, width=width),
        shape((n_head * CAP * part, width), f32),
        pos,
        inbox,
    )
    spread = lax.all_to_all(totals, "head", split_axis=0, concat_axis=0, tiled=True)
    grad_latent = call(
        functools.partial(place, part=part),
        shape((ctx_rows // n_head, width), f32),
        pos,
        spread,
    )
    return (query_grad, grad_latent)


def solution(mesh):
    return jax.shard_map(
        local,
        mesh=mesh,
        in_specs=(P("ctx", None), P("ctx", "head"), P("ctx", "head"), P("ctx", None)),
        out_specs=(P("ctx", "head"), P(("ctx", "head"), None)),
        check_vma=False,
    )
```

```python
import functools

import jax
import jax.numpy as jnp
from jax import lax
from jax.experimental import pallas as pl
from jax.experimental.pallas import tpu as pltpu
from jax.sharding import PartitionSpec as P

LAT = 512
BLOCK = 64
POOL = 36
CAP = 2
NEG = -1e30

score_scale = 192.0 ** (-0.5)
bf16 = jnp.bfloat16
f32 = jnp.float32


def iota(shape, dim):
    return lax.broadcasted_iota(jnp.int32, shape, dim)


def by20(x):
    return (x * 3277) >> 16


def dot(a, b, ca, cb):
    return lax.dot_general(a, b, (((ca,), (cb,)), ((), ())), preferred_element_type=f32)


def call(body, out_shape, *args, scratch=(), flops=0, traffic=0, mib=16):
    vmem = pl.BlockSpec(memory_space=pltpu.VMEM)
    smem = pl.BlockSpec(memory_space=pltpu.SMEM)
    specs = [smem if a.dtype == jnp.int32 and a.ndim == 1 else vmem for a in args]
    return pl.pallas_call(
        body,
        out_shape=out_shape,
        in_specs=specs,
        out_specs=jax.tree.map(lambda _: vmem, out_shape),
        scratch_shapes=list(scratch),
        compiler_params=pltpu.CompilerParams(vmem_limit_bytes=mib * 1024 * 1024),
        cost_estimate=pl.CostEstimate(flops=flops, bytes_accessed=traffic, transcendentals=0),
    )(*args)


def part_of(head):
    return head & 7


def near(head, core_flip, step):
    z = head >> 1
    core = (head & 1) ^ core_flip
    return 2 * ((z + step) & 3) + core


def choose(picks_ref, hit_ref, info_ref, ask_ref, *, per_owner):
    picks, queries = picks_ref.shape
    blocks = hit_ref.shape[0]
    block = iota((blocks, queries), 0)
    hit = jnp.zeros((blocks, queries), jnp.bool_)
    for k in range(picks):
        hit = jnp.logical_or(hit, picks_ref[k : k + 1, :] == block)
    hit = jnp.where(hit, 1.0, 0.0).astype(bf16)
    hit_ref[...] = hit
    count = dot(jnp.ones((8, queries), bf16), hit, 1, 1)
    chosen = jnp.where(count > 0.5, 1.0, 0.0)
    lo, hi = iota((blocks, blocks), 0), iota((blocks, blocks), 1)
    same = jnp.logical_and(lo < hi, by20(lo) == by20(hi))
    rank = dot(chosen.astype(bf16), jnp.where(same, 1.0, 0.0).astype(bf16), 1, 0)
    info_ref[0:8, :] = chosen
    info_ref[8:16, :] = rank
    chosen, rank = chosen[:1], rank[:1]
    rows = ask_ref.shape[0]
    row, col = iota((rows, blocks), 0), iota((rows, blocks), 1)
    key = jnp.where(chosen > 0.5, by20(col[:1]) * CAP + rank.astype(jnp.int32), -1)
    local_id = (col[:1] - by20(col[:1]) * per_owner).astype(f32)
    ask = jnp.sum(jnp.where((row >> 3) == key, local_id, 0.0), axis=1, keepdims=True)
    ask_ref[...] = jnp.broadcast_to(ask, ask_ref.shape).astype(bf16)


def arrange(pos_ref, hit_ref, info_ref, bias_ref, send_ref, *, part, first):
    blocks, queries = hit_ref.shape
    rows = send_ref.shape[0]
    chosen8 = info_ref[0:8, :]
    chosen = chosen8[:1]
    rank = info_ref[8:9, :]
    lo, hi = iota((blocks, blocks), 0), iota((blocks, blocks), 1)
    before = jnp.where(lo < hi, 1.0, 0.0).astype(bf16)
    order = dot(chosen8.astype(bf16), before, 1, 0)[:1]
    row = iota((rows, blocks), 0)
    slot = (row >> 3).astype(f32)
    here = jnp.where(jnp.logical_and(order == slot, chosen > 0.5), 1.0, 0.0)
    block_id = jnp.sum(here * iota((rows, blocks), 1).astype(f32), axis=1, keepdims=True)
    block_rank = jnp.sum(here * rank, axis=1, keepdims=True)
    block_id = block_id.astype(jnp.int32)
    block_rank = block_rank.astype(jnp.int32)
    picked = dot(here.astype(bf16), hit_ref[...], 1, 0)
    query_pos = first + pos_ref[0] * queries + iota((rows, queries), 1)
    base = block_id * BLOCK + (iota((rows, queries), 0) & 7) - query_pos
    piece = 0
    for flip in (0, 1):
        for step in (0, -1, 1, 2):
            p = near(pos_ref[1], flip, step)
            allowed = jnp.logical_and(picked > 0.5, base + p * part <= 0)
            bias_ref[piece * rows : (piece + 1) * rows, :] = jnp.where(allowed, 0.0, NEG)
            piece += 1
    row = iota(send_ref.shape, 0)
    col = iota(send_ref.shape, 1)
    target = (by20(block_id) * CAP + block_rank) * part + (row & 7)
    send_ref[...] = jnp.where(col == target, 1.0, 0.0).astype(bf16)


def fetch(pos_ref, ask_ref, lat_ref, out_ref, *, part):
    rows, tokens = out_ref.shape[0], lat_ref.shape[0]
    row, col = iota((rows, tokens), 0), iota((rows, tokens), 1)
    want = ask_ref[:, :1].astype(f32).astype(jnp.int32) * BLOCK
    want = want + part_of(pos_ref[1]) * part + (row & 7)
    pick = jnp.where(col == want, 1.0, 0.0).astype(bf16)
    out_ref[...] = dot(pick, lat_ref[...], 1, 0).astype(bf16)


def compact(send_ref, all_ref, out_ref):
    out_ref[...] = dot(send_ref[...], all_ref[...], 1, 0).astype(bf16)


def attend(
    ka_ref, kb_ref, q_ref, g_ref, bias_ref, da_ref, db_ref, ds_ref, s_ref, d_ref, qs_ref, gs_ref
):
    half, width = ka_ref.shape
    queries = q_ref.shape[0]
    heads = g_ref.shape[1] // LAT
    cols = heads * queries
    step = 384
    steps = half // step
    for h in range(heads):
        qs_ref[h * queries : (h + 1) * queries, :] = q_ref[:, h * width : (h + 1) * width]
        gs_ref[h * queries : (h + 1) * queries, :] = g_ref[:, h * LAT : (h + 1) * LAT]
    pieces = ((ka_ref, da_ref, 0), (kb_ref, db_ref, half))

    def fold(x):
        return jnp.sum(x.reshape(step // 8, 8, cols), axis=0)

    top = jnp.full((8, cols), -jnp.inf, f32)
    for k_ref, _, base in pieces:

        def one(i, top, k_ref=k_ref, base=base):
            keys = k_ref[pl.ds(pl.multiple_of(i * step, step), step), :]
            at = pl.ds(pl.multiple_of(base + i * step, step), step)
            bias = bias_ref[at, :]
            s = dot(keys, qs_ref[...], 1, 1) * score_scale + jnp.concatenate([bias] * heads, axis=1)
            s_ref[at, :] = s
            d_ref[at, :] = dot(keys[:, :LAT], gs_ref[...], 1, 1)
            return jnp.maximum(top, jnp.max(s.reshape(step // 8, 8, cols), axis=0))

        top = lax.fori_loop(0, steps, one, top)
    top = jnp.max(top, axis=0, keepdims=True)

    def two(i, carry):
        total, mixed = carry
        at = pl.ds(pl.multiple_of(i * step, step), step)
        e = jnp.exp(s_ref[at, :] - top)
        s_ref[at, :] = e
        return total + fold(e), mixed + fold(e * d_ref[at, :])

    zero = jnp.zeros((8, cols), f32)
    total, mixed = lax.fori_loop(0, 2 * steps, two, (zero, zero))
    inv = 1.0 / jnp.sum(total, axis=0, keepdims=True)
    delta = jnp.sum(mixed, axis=0, keepdims=True) * inv
    for _, dk_ref, base in pieces:

        def three(i, carry, dk_ref=dk_ref, base=base):
            here = pl.ds(pl.multiple_of(i * step, step), step)
            at = pl.ds(pl.multiple_of(base + i * step, step), step)
            p = s_ref[at, :] * inv
            ds = (p * (d_ref[at, :] - delta)).astype(bf16)
            ds_ref[at, :] = ds
            dk = dot(ds, qs_ref[...], 1, 0) * score_scale
            dv = dot(p.astype(bf16), gs_ref[...], 1, 0)
            dk_ref[here, :LAT] = (dk[:, :LAT] + dv).astype(dk_ref.dtype)
            dk_ref[here, LAT:] = dk[:, LAT:].astype(dk_ref.dtype)
            return carry

        lax.fori_loop(0, steps, three, 0)


def query_side(ds_ref, ka_ref, kb_ref, dq_ref, dqs_ref):
    half, width = ka_ref.shape
    queries = dq_ref.shape[0]
    heads = dq_ref.shape[1] // width
    step = 384
    dqs_ref[...] = jnp.zeros_like(dqs_ref)
    for k_ref, base in ((ka_ref, 0), (kb_ref, half)):

        def one(i, carry, k_ref=k_ref, base=base):
            here = pl.ds(pl.multiple_of(i * step, step), step)
            at = pl.ds(pl.multiple_of(base + i * step, step), step)
            dqs_ref[...] += dot(ds_ref[at, :], k_ref[here, :], 0, 0)
            return carry

        lax.fori_loop(0, half // step, one, 0)
    for h in range(heads):
        part = dqs_ref[h * queries : (h + 1) * queries, :] * score_scale
        dq_ref[:, h * width : (h + 1) * width] = part.astype(bf16)


def merge(keep_ref, got_ref, down_ref, up_ref, far_ref):
    rows = down_ref.shape[0]
    for i, out_ref in enumerate((down_ref, up_ref, far_ref)):
        at = slice((i + 1) * rows, (i + 2) * rows)
        out_ref[...] = (keep_ref[at, :] + got_ref[at, :].astype(f32)).astype(bf16)


def outgoing(send_ref, keep_ref, got_ref, up_ref, down_ref, far_ref, out_ref):
    rows = up_ref.shape[0]
    total = keep_ref[:rows, :] + got_ref[:rows, :].astype(f32) + up_ref[...].astype(f32)
    total = total + down_ref[...].astype(f32) + far_ref[...].astype(f32)
    out_ref[...] = dot(send_ref[...], total.astype(bf16), 0, 0).astype(bf16)


def gather_back(pos_ref, ask_ref, in_ref, out_ref, *, per_dest):
    rows, outs = in_ref.shape[0], out_ref.shape[0]
    e = part_of(pos_ref[1])
    block = ask_ref[:, :1].astype(f32).astype(jnp.int32)
    row = iota((rows, outs), 0)
    col = iota((rows, outs), 1)
    dest = col >> 4
    start = ((per_dest * dest - e + 7) >> 3) + ((col >> 3) & 1)
    inside = 8 * start + e < per_dest * (dest + 1)
    match = jnp.logical_and(block == start, (row & 7) == (col & 7))
    match = jnp.where(jnp.logical_and(match, inside), 1.0, 0.0).astype(bf16)
    out_ref[...] = dot(match, in_ref[...], 0, 0).astype(out_ref.dtype)


def place(pos_ref, in_ref, out_ref, *, per_dest):
    outs, rows = out_ref.shape[0], in_ref.shape[0]
    mine = pos_ref[1]
    row = iota((outs, rows), 0)
    col = iota((outs, rows), 1)
    e = part_of(col >> 4)
    start = ((per_dest * mine - e + 7) >> 3) + ((col >> 3) & 1)
    match = jnp.logical_and(8 * start + e == per_dest * mine + (row >> 3), (row & 7) == (col & 7))
    match = jnp.where(match, 1.0, 0.0).astype(bf16)
    out_ref[...] = dot(match, in_ref[...], 1, 0)


def local(latent, query, grad_out, picks):
    n_ctx = lax.axis_size("ctx")
    n_head = lax.axis_size("head")
    ctx_rows, width = latent.shape
    queries = query.shape[0]
    per_owner = ctx_rows // BLOCK
    blocks = per_owner * n_ctx
    part = 8
    pool_rows = POOL * part
    slots = n_ctx * CAP * part
    pos = jnp.stack([lax.axis_index("ctx"), lax.axis_index("head")]).astype(jnp.int32)
    first = (ctx_rows - queries) * n_ctx
    per_dest = ctx_rows // n_head // part
    shape = jax.ShapeDtypeStruct
    up = [(i, (i + 2) % n_head) for i in range(n_head)]
    down = [(i, (i - 2) % n_head) for i in range(n_head)]
    across = [(i, (i + 4 - 8 * (i & 1)) % n_head) for i in range(n_head)]
    twin = [(i, i ^ 1) for i in range(n_head)]

    def swap_ctx(x):
        return lax.all_to_all(
            x.reshape(n_ctx, -1, x.shape[1]), "ctx", split_axis=0, concat_axis=0, tiled=True
        ).reshape(x.shape)

    hit, info, ask = call(
        functools.partial(choose, per_owner=per_owner),
        (shape((blocks, queries), bf16), shape((16, blocks), f32), shape((slots, 128), bf16)),
        picks.T,
    )
    asked = swap_ctx(ask)
    rows_out = call(
        functools.partial(fetch, part=part), shape((slots, width), bf16), pos, asked, latent
    )
    bias, send = call(
        functools.partial(arrange, part=part, first=first),
        (shape((POOL * BLOCK, queries), f32), shape((pool_rows, slots), bf16)),
        pos,
        hit,
        info,
        flops=3 * 10**9,
        traffic=3 * 10**6,
    )
    rows_in = swap_ctx(rows_out)
    mine = call(compact, shape((pool_rows, width), bf16), send, rows_in)
    from_below = lax.ppermute(mine, "head", up)
    from_above = lax.ppermute(mine, "head", down)
    from_far = lax.ppermute(mine, "head", across)
    half = POOL * BLOCK // 2
    keys = jnp.stack([mine, from_below, from_above, from_far])
    twin_keys = lax.ppermute(keys, "head", twin).reshape(half, width)
    keys = keys.reshape(half, width)
    rows = queries * (grad_out.shape[1] // LAT)
    keep, give, score_grad = call(
        attend,
        (
            shape((half, width), f32),
            shape((half, width), bf16),
            shape((2 * half, rows), bf16),
        ),
        keys,
        twin_keys,
        query,
        grad_out,
        bias,
        scratch=(
            pltpu.VMEM((2 * half, rows), f32),
            pltpu.VMEM((2 * half, rows), f32),
            pltpu.VMEM((rows, width), bf16),
            pltpu.VMEM((rows, LAT), bf16),
        ),
        flops=6 * 10**9,
        traffic=10**7,
        mib=24,
    )
    got = lax.ppermute(give.reshape(4, pool_rows, width), "head", twin).reshape(half, width)
    piece = shape((pool_rows, width), bf16)
    to_down, to_up, to_far = call(merge, (piece, piece, piece), keep, got)
    sum_up = lax.ppermute(to_up, "head", up)
    sum_down = lax.ppermute(to_down, "head", down)
    sum_far = lax.ppermute(to_far, "head", across)
    query_grad = call(
        query_side,
        shape(query.shape, bf16),
        score_grad,
        keys,
        twin_keys,
        scratch=(pltpu.VMEM((rows, width), f32),),
        flops=3 * 10**9,
        traffic=10**7,
    )
    outbox = call(
        outgoing, shape((slots, width), bf16), send, keep, got, sum_up, sum_down, sum_far
    )
    inbox = swap_ctx(outbox)
    totals = call(
        functools.partial(gather_back, per_dest=per_dest),
        shape((n_head * CAP * part, width), bf16),
        pos,
        asked,
        inbox,
    )
    spread = lax.all_to_all(
        totals.reshape(n_head, CAP * part, width), "head", split_axis=0, concat_axis=0, tiled=True
    ).reshape(totals.shape)
    grad_latent = call(
        functools.partial(place, per_dest=per_dest),
        shape((ctx_rows // n_head, width), f32),
        pos,
        spread,
    )
    return (query_grad, grad_latent)


def solution(mesh):
    return jax.shard_map(
        local,
        mesh=mesh,
        in_specs=(P("ctx", None), P("ctx", "head"), P("ctx", "head"), P("ctx", None)),
        out_specs=(P("ctx", "head"), P(("ctx", "head"), None)),
        check_vma=False,
    )
```

```python
import functools

import jax
import jax.numpy as jnp
from jax import lax
from jax.experimental import pallas as pl
from jax.experimental.pallas import tpu as pltpu
from jax.sharding import PartitionSpec as P

LAT = 512
BLOCK = 64
POOL = 36
CAP = 2
NEG = -1e30

score_scale = 192.0 ** (-0.5)
bf16 = jnp.bfloat16
f32 = jnp.float32


def iota(shape, dim):
    return lax.broadcasted_iota(jnp.int32, shape, dim)


def by20(x):
    return (x * 3277) >> 16


def dot(a, b, ca, cb):
    return lax.dot_general(a, b, (((ca,), (cb,)), ((), ())), preferred_element_type=f32)


def call(body, out_shape, *args, scratch=(), flops=0, traffic=0, mib=16):
    vmem = pl.BlockSpec(memory_space=pltpu.VMEM)
    smem = pl.BlockSpec(memory_space=pltpu.SMEM)
    specs = [smem if a.dtype == jnp.int32 and a.ndim == 1 else vmem for a in args]
    return pl.pallas_call(
        body,
        out_shape=out_shape,
        in_specs=specs,
        out_specs=jax.tree.map(lambda _: vmem, out_shape),
        scratch_shapes=list(scratch),
        compiler_params=pltpu.CompilerParams(vmem_limit_bytes=mib * 1024 * 1024),
        cost_estimate=pl.CostEstimate(flops=flops, bytes_accessed=traffic, transcendentals=0),
    )(*args)


PART = 8
LINES = 4


def part_of(head):
    return head & 7


def near(head, core_flip, step):
    z = head >> 1
    core = (head & 1) ^ core_flip
    return 2 * ((z + step) & 3) + core


def one_hot(mask):
    return jnp.where(mask, 1.0, 0.0).astype(bf16)


def own_part(pos_ref, lat_ref, out_ref):
    rows, tokens, width = out_ref.shape[0], lat_ref.shape[0], lat_ref.shape[1]
    row, col = iota((rows, tokens), 0), iota((rows, tokens), 1)
    want = (row >> 2) * BLOCK + part_of(pos_ref[1]) * PART + (row & 3)
    for u in (0, 1):
        lines = dot(one_hot(col == want + u * LINES), lat_ref[...], 1, 0)
        out_ref[:, u * width : (u + 1) * width] = lines.astype(bf16)


def choose(picks_ref, hit_ref, info_ref, ask_ref, *, per_owner):
    picks, queries = picks_ref.shape
    blocks = hit_ref.shape[0]
    block = iota((blocks, queries), 0)
    hit = jnp.zeros((blocks, queries), jnp.bool_)
    for k in range(picks):
        hit = jnp.logical_or(hit, picks_ref[k : k + 1, :] == block)
    hit = one_hot(hit)
    hit_ref[...] = hit
    count = dot(jnp.ones((8, queries), bf16), hit, 1, 1)
    chosen = jnp.where(count > 0.5, 1.0, 0.0)
    lo, hi = iota((blocks, blocks), 0), iota((blocks, blocks), 1)
    same = jnp.logical_and(lo < hi, lo >= by20(hi[:1]) * per_owner)
    rank = dot(chosen.astype(bf16), one_hot(same), 1, 0)
    info_ref[0:8, :] = chosen
    info_ref[8:16, :] = rank
    chosen, rank = chosen[:1], rank[:1]
    rows = ask_ref.shape[0]
    row, col = iota((rows, blocks), 0), iota((1, blocks), 1)
    key = jnp.where(chosen > 0.5, by20(col) * CAP + rank.astype(jnp.int32), -1)
    local_id = (col - by20(col) * per_owner).astype(f32)
    ask = jnp.sum(jnp.where((row >> 2) == key, local_id, 0.0), axis=1, keepdims=True)
    ask_ref[...] = jnp.broadcast_to(ask, ask_ref.shape).astype(bf16)


def fetch(ask_ref, own_ref, out_ref):
    rows, lines = out_ref.shape[0], own_ref.shape[0]
    row, col = iota((rows, lines), 0), iota((rows, lines), 1)
    want = ask_ref[:, :1].astype(f32).astype(jnp.int32) * LINES + (row & 3)
    out_ref[...] = dot(one_hot(col == want), own_ref[...], 1, 0).astype(bf16)


def arrange(
    pos_ref, hit_ref, info_ref, ask_ref, bias_ref, send_ref, back_ref, sum_ref, place_ref, *, first, per_dest
):
    blocks, queries = hit_ref.shape
    rows, slots = send_ref.shape
    head = pos_ref[1]
    chosen8 = info_ref[0:8, :]
    chosen = chosen8[:1]
    rank = info_ref[8:9, :]
    lo, hi = iota((blocks, blocks), 0), iota((blocks, blocks), 1)
    order = dot(chosen8.astype(bf16), one_hot(lo < hi), 1, 0)[:1]
    row = iota((rows, blocks), 0)
    slot = (row >> 2).astype(f32)
    here = jnp.where(jnp.logical_and(order == slot, chosen > 0.5), 1.0, 0.0)
    block_id = jnp.sum(here * iota((rows, blocks), 1).astype(f32), axis=1, keepdims=True)
    block_rank = jnp.sum(here * rank, axis=1, keepdims=True)
    block_id = block_id.astype(jnp.int32)
    block_rank = block_rank.astype(jnp.int32)
    picked = dot(here.astype(bf16), hit_ref[...], 1, 0)
    query_pos = first + pos_ref[0] * queries + iota((rows, queries), 1)
    base = block_id * BLOCK + (iota((rows, queries), 0) & 3) - query_pos
    piece = 0
    for flip in (0, 1):
        for u in (0, 1):
            for step in (0, -1, 1, 2):
                offset = near(head, flip, step) * PART + u * LINES
                allowed = jnp.logical_and(picked > 0.5, base + offset <= 0)
                bias_ref[piece * rows : (piece + 1) * rows, :] = jnp.where(allowed, 0.0, NEG)
                piece += 1
    row = iota(send_ref.shape, 0)
    col = iota(send_ref.shape, 1)
    send = one_hot(col == (by20(block_id) * CAP + block_rank) * LINES + (row & 3))
    send_ref[...] = send
    unit = one_hot(iota((rows, rows), 0) == iota((rows, rows), 1))
    back_ref[...] = dot(send, unit, 0, 0).astype(bf16)
    ids = dot(one_hot(iota((8, 128), 1) == 0), ask_ref[...], 1, 1)[:1].astype(jnp.int32)
    row = iota(sum_ref.shape, 0)
    col = iota(sum_ref.shape, 1)
    e = part_of(head)
    dest = row >> 3
    start = ((per_dest * dest - e + 7) >> 3) + ((row >> 2) & 1)
    inside = 8 * start + e < per_dest * (dest + 1)
    match = jnp.logical_and(ids == start, (row & 3) == (col & 3))
    sum_ref[...] = one_hot(jnp.logical_and(match, inside))
    outs = place_ref.shape[0] // 2
    row = iota((outs, place_ref.shape[1]), 0)
    col = iota((outs, place_ref.shape[1]), 1)
    e = part_of(col >> 3)
    start = ((per_dest * head - e + 7) >> 3) + ((col >> 2) & 1)
    match = jnp.logical_and(8 * start + e == per_dest * head + (row >> 3), (row & 3) == (col & 3))
    for u in (0, 1):
        mine = jnp.logical_and(match, ((row >> 2) & 1) == u)
        place_ref[u * outs : (u + 1) * outs, :] = one_hot(mine)


def multiply(a_ref, b_ref, out_ref):
    out_ref[...] = dot(a_ref[...], b_ref[...], 1, 0).astype(out_ref.dtype)


def attend(
    ka_ref, kb_ref, q_ref, g_ref, bias_ref, keep_ref, give_ref, ds_ref, k_ref, s_ref, d_ref, qs_ref, gs_ref
):
    tokens, width = k_ref.shape
    queries = q_ref.shape[0]
    heads = g_ref.shape[1] // LAT
    cols = heads * queries
    quarter = tokens // 4
    for i, (piece_ref, u) in enumerate(((ka_ref, 0), (ka_ref, 1), (kb_ref, 0), (kb_ref, 1))):
        k_ref[i * quarter : (i + 1) * quarter, :] = piece_ref[:, u * width : (u + 1) * width]
    for h in range(heads):
        qs_ref[h * queries : (h + 1) * queries, :] = q_ref[:, h * width : (h + 1) * width]
        gs_ref[h * queries : (h + 1) * queries, :] = g_ref[:, h * LAT : (h + 1) * LAT]
    step = 384

    def fold(x):
        return jnp.sum(x.reshape(step // 8, 8, cols), axis=0)

    def one(i, top):
        at = pl.ds(pl.multiple_of(i * step, step), step)
        keys = k_ref[at, :]
        bias = bias_ref[at, :]
        s = dot(keys, qs_ref[...], 1, 1) * score_scale + jnp.concatenate([bias] * heads, axis=1)
        s_ref[at, :] = s
        d_ref[at, :] = dot(keys[:, :LAT], gs_ref[...], 1, 1)
        return jnp.maximum(top, jnp.max(s.reshape(step // 8, 8, cols), axis=0))

    top = lax.fori_loop(0, tokens // step, one, jnp.full((8, cols), -jnp.inf, f32))
    top = jnp.max(top, axis=0, keepdims=True)

    def two(i, carry):
        total, mixed = carry
        at = pl.ds(pl.multiple_of(i * step, step), step)
        e = jnp.exp(s_ref[at, :] - top)
        s_ref[at, :] = e
        return total + fold(e), mixed + fold(e * d_ref[at, :])

    zero = jnp.zeros((8, cols), f32)
    total, mixed = lax.fori_loop(0, tokens // step, two, (zero, zero))
    inv = 1.0 / jnp.sum(total, axis=0, keepdims=True)
    delta = jnp.sum(mixed, axis=0, keepdims=True) * inv
    less = quarter // 2
    for i, (out_ref, u) in enumerate(((keep_ref, 0), (keep_ref, 1), (give_ref, 0), (give_ref, 1))):

        def three(j, carry, i=i, out_ref=out_ref, u=u):
            here = pl.ds(pl.multiple_of(j * less, less), less)
            at = pl.ds(pl.multiple_of(i * quarter + j * less, less), less)
            p = s_ref[at, :] * inv
            ds = (p * (d_ref[at, :] - delta)).astype(bf16)
            ds_ref[at, :] = ds
            dk = dot(ds, qs_ref[...], 1, 0) * score_scale
            dv = dot(p.astype(bf16), gs_ref[...], 1, 0)
            both = jnp.concatenate([dk[:, :LAT] + dv, dk[:, LAT:]], axis=1)
            out_ref[here, u * width : (u + 1) * width] = both.astype(out_ref.dtype)
            return carry

        lax.fori_loop(0, 2, three, 0)


def query_side(ds_ref, k_ref, dq_ref, dqs_ref):
    tokens, width = k_ref.shape
    queries = dq_ref.shape[0]
    heads = dq_ref.shape[1] // width
    step = 768
    dqs_ref[...] = jnp.zeros_like(dqs_ref)

    def one(i, carry):
        at = pl.ds(pl.multiple_of(i * step, step), step)
        dqs_ref[...] += dot(ds_ref[at, :], k_ref[at, :], 0, 0)
        return carry

    lax.fori_loop(0, tokens // step, one, 0)
    for h in range(heads):
        part = dqs_ref[h * queries : (h + 1) * queries, :] * score_scale
        dq_ref[:, h * width : (h + 1) * width] = part.astype(bf16)


def merge(keep_ref, got_ref, down_ref, up_ref, far_ref):
    rows = down_ref.shape[0]
    for i, out_ref in enumerate((down_ref, up_ref, far_ref)):
        at = slice((i + 1) * rows, (i + 2) * rows)
        out_ref[...] = (keep_ref[at, :] + got_ref[at, :].astype(f32)).astype(bf16)


def outgoing(back_ref, keep_ref, got_ref, up_ref, down_ref, far_ref, out_ref):
    rows = up_ref.shape[0]
    total = keep_ref[:rows, :] + got_ref[:rows, :].astype(f32) + up_ref[...].astype(f32)
    total = total + down_ref[...].astype(f32) + far_ref[...].astype(f32)
    out_ref[...] = dot(back_ref[...], total.astype(bf16), 1, 0).astype(bf16)


def place(place_ref, in_ref, out_ref):
    outs, width = out_ref.shape
    first = dot(place_ref[:outs, :], in_ref[:, :width], 1, 0)
    out_ref[...] = first + dot(place_ref[outs:, :], in_ref[:, width:], 1, 0)


def local(latent, query, grad_out, picks):
    n_ctx = lax.axis_size("ctx")
    n_head = lax.axis_size("head")
    ctx_rows, width = latent.shape
    queries = query.shape[0]
    per_owner = ctx_rows // BLOCK
    blocks = per_owner * n_ctx
    line = 2 * width
    pool_lines = POOL * LINES
    slots = n_ctx * CAP * LINES
    tokens = POOL * BLOCK
    outs = ctx_rows // n_head
    pos = jnp.stack([lax.axis_index("ctx"), lax.axis_index("head")]).astype(jnp.int32)
    first = (ctx_rows - queries) * n_ctx
    shape = jax.ShapeDtypeStruct
    up = [(i, (i + 2) % n_head) for i in range(n_head)]
    down = [(i, (i - 2) % n_head) for i in range(n_head)]
    across = [(i, (i + 4 - 8 * (i & 1)) % n_head) for i in range(n_head)]
    twin = [(i, i ^ 1) for i in range(n_head)]

    def swap(x, axis):
        n = lax.axis_size(axis)
        x3 = x.reshape(n, -1, x.shape[1])
        return lax.all_to_all(x3, axis, split_axis=0, concat_axis=0, tiled=True).reshape(x.shape)

    hit, info, ask = call(
        functools.partial(choose, per_owner=per_owner),
        (shape((blocks, queries), bf16), shape((16, blocks), f32), shape((slots, 128), bf16)),
        picks.T,
    )
    own = call(own_part, shape((per_owner * LINES, line), bf16), pos, latent, flops=10**9, traffic=10**6)
    asked = swap(ask, "ctx")
    lines_out = call(fetch, shape((slots, line), bf16), asked, own)
    bias, send, back, sums, places = call(
        functools.partial(arrange, first=first, per_dest=outs // PART),
        (
            shape((tokens, queries), f32),
            shape((pool_lines, slots), bf16),
            shape((slots, pool_lines), bf16),
            shape((n_head * CAP * LINES, slots), bf16),
            shape((2 * outs, n_head * CAP * LINES), bf16),
        ),
        pos,
        hit,
        info,
        asked,
        flops=3 * 10**9,
        traffic=3 * 10**6,
    )
    lines_in = swap(lines_out, "ctx")
    mine = call(multiply, shape((pool_lines, line), bf16), send, lines_in)
    from_below = lax.ppermute(mine, "head", up)
    from_above = lax.ppermute(mine, "head", down)
    from_far = lax.ppermute(mine, "head", across)
    keys = jnp.stack([mine, from_below, from_above, from_far])
    twin_keys = lax.ppermute(keys, "head", twin).reshape(4 * pool_lines, line)
    keys = keys.reshape(4 * pool_lines, line)
    rows = queries * (grad_out.shape[1] // LAT)
    keep, give, score_grad, all_keys = call(
        attend,
        (
            shape((4 * pool_lines, line), f32),
            shape((4 * pool_lines, line), bf16),
            shape((tokens, rows), bf16),
            shape((tokens, width), bf16),
        ),
        keys,
        twin_keys,
        query,
        grad_out,
        bias,
        scratch=(
            pltpu.VMEM((tokens, rows), f32),
            pltpu.VMEM((tokens, rows), f32),
            pltpu.VMEM((rows, width), bf16),
            pltpu.VMEM((rows, LAT), bf16),
        ),
        flops=6 * 10**9,
        traffic=10**7,
        mib=24,
    )
    got = lax.ppermute(give.reshape(4, pool_lines, line), "head", twin)
    got = got.reshape(4 * pool_lines, line)
    piece = shape((pool_lines, line), bf16)
    to_down, to_up, to_far = call(merge, (piece, piece, piece), keep, got)
    sum_up = lax.ppermute(to_up, "head", up)
    sum_down = lax.ppermute(to_down, "head", down)
    sum_far = lax.ppermute(to_far, "head", across)
    query_grad = call(
        query_side,
        shape(query.shape, bf16),
        score_grad,
        all_keys,
        scratch=(pltpu.VMEM((rows, width), f32),),
        flops=3 * 10**9,
        traffic=10**7,
    )
    outbox = call(
        outgoing, shape((slots, line), bf16), back, keep, got, sum_up, sum_down, sum_far
    )
    inbox = swap(outbox, "ctx")
    totals = call(multiply, shape((n_head * CAP * LINES, line), bf16), sums, inbox)
    spread = swap(totals, "head")
    grad_latent = call(place, shape((outs, width), f32), places, spread)
    return (query_grad, grad_latent)


def solution(mesh):
    return jax.shard_map(
        local,
        mesh=mesh,
        in_specs=(P("ctx", None), P("ctx", "head"), P("ctx", "head"), P("ctx", None)),
        out_specs=(P("ctx", "head"), P(("ctx", "head"), None)),
        check_vma=False,
    )
```

```python
import functools

import jax
import jax.numpy as jnp
from jax import lax
from jax.experimental import pallas as pl
from jax.experimental.pallas import tpu as pltpu
from jax.sharding import PartitionSpec as P

LAT = 512
BLOCK = 64
POOL = 36
CAP = 2
NEG = -1e30

score_scale = 192.0 ** (-0.5)
bf16 = jnp.bfloat16
f32 = jnp.float32


def iota(shape, dim):
    return lax.broadcasted_iota(jnp.int32, shape, dim)


def by20(x):
    return (x * 3277) >> 16


def dot(a, b, ca, cb):
    return lax.dot_general(a, b, (((ca,), (cb,)), ((), ())), preferred_element_type=f32)


def call(body, out_shape, *args, scratch=(), flops=0, traffic=0, mib=16):
    vmem = pl.BlockSpec(memory_space=pltpu.VMEM)
    smem = pl.BlockSpec(memory_space=pltpu.SMEM)
    specs = [smem if a.dtype == jnp.int32 and a.ndim == 1 else vmem for a in args]
    return pl.pallas_call(
        body,
        out_shape=out_shape,
        in_specs=specs,
        out_specs=jax.tree.map(lambda _: vmem, out_shape),
        scratch_shapes=list(scratch),
        compiler_params=pltpu.CompilerParams(vmem_limit_bytes=mib * 1024 * 1024),
        cost_estimate=pl.CostEstimate(flops=flops, bytes_accessed=traffic, transcendentals=0),
    )(*args)


PART = 8
LINES = 4


def part_of(head):
    return head & 7


def near(head, step):
    return 2 * (((head >> 1) + step) & 3) + (head & 1)


def one_hot(mask):
    return jnp.where(mask, 1.0, 0.0).astype(bf16)


def own_part(pos_ref, lat_ref, out_ref):
    rows, tokens, width = out_ref.shape[0], lat_ref.shape[0], lat_ref.shape[1]
    row, col = iota((rows, tokens), 0), iota((rows, tokens), 1)
    want = (row >> 2) * BLOCK + part_of(pos_ref[1]) * PART + (row & 3)
    for u in (0, 1):
        lines = dot(one_hot(col == want + u * LINES), lat_ref[...], 1, 0)
        out_ref[:, u * width : (u + 1) * width] = lines.astype(bf16)


def choose(picks_ref, hit_ref, info_ref, ask_ref, *, per_owner):
    picks, queries = picks_ref.shape
    blocks = hit_ref.shape[0]
    block = iota((blocks, queries), 0)
    hit = jnp.zeros((blocks, queries), jnp.bool_)
    for k in range(picks):
        hit = jnp.logical_or(hit, picks_ref[k : k + 1, :] == block)
    hit = one_hot(hit)
    hit_ref[...] = hit
    count = dot(jnp.ones((8, queries), bf16), hit, 1, 1)
    chosen = jnp.where(count > 0.5, 1.0, 0.0)
    lo, hi = iota((blocks, blocks), 0), iota((blocks, blocks), 1)
    same = jnp.logical_and(lo < hi, lo >= by20(hi[:1]) * per_owner)
    rank = dot(chosen.astype(bf16), one_hot(same), 1, 0)
    info_ref[0:8, :] = chosen
    info_ref[8:16, :] = rank
    chosen, rank = chosen[:1], rank[:1]
    rows = ask_ref.shape[0]
    row, col = iota((rows, blocks), 0), iota((1, blocks), 1)
    key = jnp.where(chosen > 0.5, by20(col) * CAP + rank.astype(jnp.int32), -1)
    local_id = (col - by20(col) * per_owner).astype(f32)
    ask = jnp.sum(jnp.where((row >> 2) == key, local_id, 0.0), axis=1, keepdims=True)
    ask_ref[...] = jnp.broadcast_to(ask, ask_ref.shape).astype(bf16)


def fetch(ask_ref, own_ref, out_ref):
    rows, lines = out_ref.shape[0], own_ref.shape[0]
    row, col = iota((rows, lines), 0), iota((rows, lines), 1)
    want = ask_ref[:, :1].astype(f32).astype(jnp.int32) * LINES + (row & 3)
    out_ref[...] = dot(one_hot(col == want), own_ref[...], 1, 0).astype(bf16)


def arrange(
    pos_ref, hit_ref, info_ref, ask_ref, bias_ref, send_ref, back_ref, sum_ref, place_ref, *, first, per_dest
):
    blocks, queries = hit_ref.shape
    rows, slots = send_ref.shape
    head = pos_ref[1]
    chosen8 = info_ref[0:8, :]
    chosen = chosen8[:1]
    rank = info_ref[8:9, :]
    lo, hi = iota((blocks, blocks), 0), iota((blocks, blocks), 1)
    order = dot(chosen8.astype(bf16), one_hot(lo < hi), 1, 0)[:1]
    row = iota((rows, blocks), 0)
    slot = (row >> 2).astype(f32)
    here = jnp.where(jnp.logical_and(order == slot, chosen > 0.5), 1.0, 0.0)
    block_id = jnp.sum(here * iota((rows, blocks), 1).astype(f32), axis=1, keepdims=True)
    block_rank = jnp.sum(here * rank, axis=1, keepdims=True)
    block_id = block_id.astype(jnp.int32)
    block_rank = block_rank.astype(jnp.int32)
    picked = dot(here.astype(bf16), hit_ref[...], 1, 0)
    query_pos = first + pos_ref[0] * queries + iota((rows, queries), 1)
    base = block_id * BLOCK + (iota((rows, queries), 0) & 3) - query_pos
    piece = 0
    for u in (0, 1):
        for step in (0, -1, 1, 2):
            offset = near(head, step) * PART + u * LINES
            allowed = jnp.logical_and(picked > 0.5, base + offset <= 0)
            bias_ref[piece * rows : (piece + 1) * rows, :] = jnp.where(allowed, 0.0, NEG)
            piece += 1
    row = iota(send_ref.shape, 0)
    col = iota(send_ref.shape, 1)
    send = one_hot(col == (by20(block_id) * CAP + block_rank) * LINES + (row & 3))
    send_ref[...] = send
    unit = one_hot(iota((rows, rows), 0) == iota((rows, rows), 1))
    back_ref[...] = dot(send, unit, 0, 0).astype(bf16)
    ids = dot(one_hot(iota((8, 128), 1) == 0), ask_ref[...], 1, 1)[:1].astype(jnp.int32)
    row = iota(sum_ref.shape, 0)
    col = iota(sum_ref.shape, 1)
    e = part_of(head)
    dest = row >> 3
    start = ((per_dest * dest - e + 7) >> 3) + ((row >> 2) & 1)
    inside = 8 * start + e < per_dest * (dest + 1)
    match = jnp.logical_and(ids == start, (row & 3) == (col & 3))
    sum_ref[...] = one_hot(jnp.logical_and(match, inside))
    outs = place_ref.shape[0] // 2
    row = iota((outs, place_ref.shape[1]), 0)
    col = iota((outs, place_ref.shape[1]), 1)
    e = part_of(col >> 3)
    start = ((per_dest * head - e + 7) >> 3) + ((col >> 2) & 1)
    match = jnp.logical_and(8 * start + e == per_dest * head + (row >> 3), (row & 3) == (col & 3))
    for u in (0, 1):
        mine = jnp.logical_and(match, ((row >> 2) & 1) == u)
        place_ref[u * outs : (u + 1) * outs, :] = one_hot(mine)


def multiply(a_ref, b_ref, out_ref):
    out_ref[...] = dot(a_ref[...], b_ref[...], 1, 0).astype(out_ref.dtype)


def score(
    own_ref, below_ref, above_ref, far_ref, q_ref, g_ref, qt_ref, gt_ref, bias_ref,
    e_ref, d_ref, stat_ref, k_ref, qs_ref, gs_ref,
):
    tokens, width = k_ref.shape
    queries = q_ref.shape[0]
    heads = g_ref.shape[1] // LAT
    cols = 2 * heads * queries
    lines = own_ref.shape[0]
    for u in (0, 1):
        for i, piece_ref in enumerate((own_ref, below_ref, above_ref, far_ref)):
            at = (4 * u + i) * lines
            k_ref[at : at + lines, :] = piece_ref[:, u * width : (u + 1) * width]
    for c, (x_ref, y_ref) in enumerate(((q_ref, g_ref), (qt_ref, gt_ref))):
        for h in range(heads):
            at = (c * heads + h) * queries
            qs_ref[at : at + queries, :] = x_ref[:, h * width : (h + 1) * width]
            gs_ref[at : at + queries, :] = y_ref[:, h * LAT : (h + 1) * LAT]
    step = 384

    def fold(x):
        return jnp.sum(x.reshape(step // 8, 8, cols), axis=0)

    def one(i, top):
        at = pl.ds(pl.multiple_of(i * step, step), step)
        keys = k_ref[at, :]
        bias = jnp.concatenate([bias_ref[at, :]] * (2 * heads), axis=1)
        s = dot(keys, qs_ref[...], 1, 1) * score_scale + bias
        e_ref[at, :] = s
        d_ref[at, :] = dot(keys[:, :LAT], gs_ref[...], 1, 1)
        return jnp.maximum(top, jnp.max(s.reshape(step // 8, 8, cols), axis=0))

    top = lax.fori_loop(0, tokens // step, one, jnp.full((8, cols), -jnp.inf, f32))
    top = jnp.max(top, axis=0, keepdims=True)

    def two(i, carry):
        total, mixed = carry
        at = pl.ds(pl.multiple_of(i * step, step), step)
        e = jnp.exp(e_ref[at, :] - top)
        e_ref[at, :] = e
        return total + fold(e), mixed + fold(e * d_ref[at, :])

    zero = jnp.zeros((8, cols), f32)
    total, mixed = lax.fori_loop(0, tokens // step, two, (zero, zero))
    stat_ref[0:1, :] = top
    stat_ref[1:2, :] = jnp.sum(total, axis=0, keepdims=True)
    stat_ref[2:3, :] = jnp.sum(mixed, axis=0, keepdims=True)
    stat_ref[3:8, :] = jnp.zeros((5, cols), f32)


def key_side(
    e_ref, d_ref, stat_ref, other_ref, qs_ref, gs_ref, own_ref, down_ref, up_ref, far_ref, ds_ref
):
    tokens, cols = e_ref.shape
    width = qs_ref.shape[1]
    lines = own_ref.shape[0]
    mine = stat_ref[...]
    other = other_ref[...]
    other = jnp.concatenate([other[:, cols // 2 :], other[:, : cols // 2]], axis=1)
    top = jnp.maximum(mine[0:1], other[0:1])
    a, b = jnp.exp(mine[0:1] - top), jnp.exp(other[0:1] - top)
    inv = 1.0 / (mine[1:2] * a + other[1:2] * b)
    delta = (mine[2:3] * a + other[2:3] * b) * inv
    scale = a * inv
    outs = (own_ref, down_ref, up_ref, far_ref)
    step = 2 * lines
    for i in range(tokens // step):
        at = slice(i * step, (i + 1) * step)
        u = i // 2
        p = e_ref[at, :] * scale
        ds = (p * (d_ref[at, :] - delta)).astype(bf16)
        ds_ref[at, :] = ds
        dk = dot(ds, qs_ref[...], 1, 0) * score_scale
        dv = dot(p.astype(bf16), gs_ref[...], 1, 0)
        both = jnp.concatenate([dk[:, :LAT] + dv, dk[:, LAT:]], axis=1)
        for j in (0, 1):
            out_ref = outs[2 * (i % 2) + j]
            part = both[j * lines : (j + 1) * lines, :]
            out_ref[:, u * width : (u + 1) * width] = part.astype(out_ref.dtype)


def query_side(ds_ref, k_ref, mine_ref, other_ref, dqs_ref):
    tokens, width = k_ref.shape
    rows = mine_ref.shape[0]
    step = 384
    dqs_ref[...] = jnp.zeros_like(dqs_ref)

    def one(i, carry):
        at = pl.ds(pl.multiple_of(i * step, step), step)
        dqs_ref[...] += dot(ds_ref[at, :], k_ref[at, :], 0, 0)
        return carry

    lax.fori_loop(0, tokens // step, one, 0)
    for i, out_ref in enumerate((mine_ref, other_ref)):
        for u in (0, 1):
            at = (2 * i + u) * rows
            out_ref[:, u * width : (u + 1) * width] = dqs_ref[at : at + rows, :]


def query_sum(mine_ref, got_ref, dq_ref):
    queries = dq_ref.shape[0]
    heads, line = mine_ref.shape[0] // queries, mine_ref.shape[1]
    width = line // 2
    for h in range(heads):
        at = slice(h * queries, (h + 1) * queries)
        total = ((mine_ref[at, :] + got_ref[at, :]) * score_scale).astype(bf16)
        dq_ref[:, h * width : (h + 1) * width] = total[:, :width]
        h2 = h + heads
        dq_ref[:, h2 * width : (h2 + 1) * width] = total[:, width:]


def outgoing(back_ref, own_ref, up_ref, down_ref, far_ref, out_ref):
    total = own_ref[...] + up_ref[...].astype(f32)
    total = total + down_ref[...].astype(f32) + far_ref[...].astype(f32)
    out_ref[...] = dot(back_ref[...], total.astype(bf16), 1, 0).astype(bf16)


def place(place_ref, in_ref, out_ref):
    outs, width = out_ref.shape
    first = dot(place_ref[:outs, :], in_ref[:, :width], 1, 0)
    out_ref[...] = first + dot(place_ref[outs:, :], in_ref[:, width:], 1, 0)


def local(latent, query, grad_out, picks):
    n_ctx = lax.axis_size("ctx")
    n_head = lax.axis_size("head")
    ctx_rows, width = latent.shape
    queries = query.shape[0]
    per_owner = ctx_rows // BLOCK
    blocks = per_owner * n_ctx
    line = 2 * width
    pool_lines = POOL * LINES
    slots = n_ctx * CAP * LINES
    tokens = POOL * BLOCK // 2
    outs = ctx_rows // n_head
    pos = jnp.stack([lax.axis_index("ctx"), lax.axis_index("head")]).astype(jnp.int32)
    first = (ctx_rows - queries) * n_ctx
    shape = jax.ShapeDtypeStruct
    up = [(i, (i + 2) % n_head) for i in range(n_head)]
    down = [(i, (i - 2) % n_head) for i in range(n_head)]
    across = [(i, (i + 4 - 8 * (i & 1)) % n_head) for i in range(n_head)]
    twin = [(i, i ^ 1) for i in range(n_head)]

    def swap(x, axis):
        n = lax.axis_size(axis)
        x3 = x.reshape(n, -1, x.shape[1])
        return lax.all_to_all(x3, axis, split_axis=0, concat_axis=0, tiled=True).reshape(x.shape)

    hit, info, ask = call(
        functools.partial(choose, per_owner=per_owner),
        (shape((blocks, queries), bf16), shape((16, blocks), f32), shape((slots, 128), bf16)),
        picks.T,
    )
    own = call(own_part, shape((per_owner * LINES, line), bf16), pos, latent, flops=10**9, traffic=10**6)
    asked = swap(ask, "ctx")
    lines_out = call(fetch, shape((slots, line), bf16), asked, own)
    bias, send, back, sums, places = call(
        functools.partial(arrange, first=first, per_dest=outs // PART),
        (
            shape((tokens, queries), f32),
            shape((pool_lines, slots), bf16),
            shape((slots, pool_lines), bf16),
            shape((n_head * CAP * LINES, slots), bf16),
            shape((2 * outs, n_head * CAP * LINES), bf16),
        ),
        pos,
        hit,
        info,
        asked,
        flops=3 * 10**9,
        traffic=3 * 10**6,
    )
    query, grad_out, bias = lax.optimization_barrier((query, grad_out, bias))
    twin_query = lax.ppermute(query, "head", twin)
    twin_grad = lax.ppermute(grad_out, "head", twin)
    lines_in = swap(lines_out, "ctx")
    mine = call(multiply, shape((pool_lines, line), bf16), send, lines_in)
    from_below = lax.ppermute(mine, "head", up)
    from_above = lax.ppermute(mine, "head", down)
    from_far = lax.ppermute(mine, "head", across)
    rows = queries * (grad_out.shape[1] // LAT)
    scores, prob_grad, stats, keys, query_rows, grad_rows = call(
        score,
        (
            shape((tokens, 2 * rows), f32),
            shape((tokens, 2 * rows), f32),
            shape((8, 2 * rows), f32),
            shape((tokens, width), bf16),
            shape((2 * rows, width), bf16),
            shape((2 * rows, LAT), bf16),
        ),
        mine,
        from_below,
        from_above,
        from_far,
        query,
        grad_out,
        twin_query,
        twin_grad,
        bias,
        flops=3 * 10**9,
        traffic=10**7,
        mib=20,
    )
    twin_stats = lax.ppermute(stats, "head", twin)
    piece = shape((pool_lines, line), bf16)
    to_own, to_down, to_up, to_far, score_grad = call(
        key_side,
        (shape((pool_lines, line), f32), piece, piece, piece, shape((tokens, 2 * rows), bf16)),
        scores,
        prob_grad,
        stats,
        twin_stats,
        query_rows,
        grad_rows,
        flops=3 * 10**9,
        traffic=10**7,
        mib=20,
    )
    sum_up = lax.ppermute(to_up, "head", up)
    sum_down = lax.ppermute(to_down, "head", down)
    sum_far = lax.ppermute(to_far, "head", across)
    half_grad = shape((rows // 2, line), f32)
    query_mine, query_other = call(
        query_side,
        (half_grad, half_grad),
        score_grad,
        keys,
        scratch=(pltpu.VMEM((2 * rows, width), f32),),
        flops=3 * 10**9,
        traffic=10**7,
    )
    query_got = lax.ppermute(query_other, "head", twin)
    query_grad = call(query_sum, shape(query.shape, bf16), query_mine, query_got)
    outbox = call(outgoing, shape((slots, line), bf16), back, to_own, sum_up, sum_down, sum_far)
    inbox = swap(outbox, "ctx")
    totals = call(multiply, shape((n_head * CAP * LINES, line), bf16), sums, inbox)
    spread = swap(totals, "head")
    grad_latent = call(place, shape((outs, width), f32), places, spread)
    return (query_grad, grad_latent)


def solution(mesh):
    return jax.shard_map(
        local,
        mesh=mesh,
        in_specs=(P("ctx", None), P("ctx", "head"), P("ctx", "head"), P("ctx", None)),
        out_specs=(P("ctx", "head"), P(("ctx", "head"), None)),
        check_vma=False,
    )
```

```python
import functools

import jax
import jax.numpy as jnp
from jax import lax
from jax.experimental import pallas as pl
from jax.experimental.pallas import tpu as pltpu
from jax.sharding import PartitionSpec as P

LAT = 512
BLOCK = 64
POOL = 36
CAP = 2
NEG = -1e30

score_scale = 192.0 ** (-0.5)
bf16 = jnp.bfloat16
f32 = jnp.float32


def iota(shape, dim):
    return lax.broadcasted_iota(jnp.int32, shape, dim)


def by20(x):
    return (x * 3277) >> 16


def dot(a, b, ca, cb):
    return lax.dot_general(a, b, (((ca,), (cb,)), ((), ())), preferred_element_type=f32)


def call(body, out_shape, *args, scratch=(), flops=0, traffic=0, mib=16, hbm=()):
    vmem = pl.BlockSpec(memory_space=pltpu.VMEM)
    smem = pl.BlockSpec(memory_space=pltpu.SMEM)
    specs = [smem if a.dtype == jnp.int32 and a.ndim == 1 else vmem for a in args]
    for i in hbm:
        specs[i] = pl.BlockSpec(memory_space=pl.ANY)
    return pl.pallas_call(
        body,
        out_shape=out_shape,
        in_specs=specs,
        out_specs=jax.tree.map(lambda _: vmem, out_shape),
        scratch_shapes=list(scratch),
        compiler_params=pltpu.CompilerParams(vmem_limit_bytes=mib * 1024 * 1024),
        cost_estimate=pl.CostEstimate(flops=flops, bytes_accessed=traffic, transcendentals=0),
    )(*args)


PART = 8
LINES = 4


def part_of(head):
    return head & 7


def near(head, step):
    return 2 * (((head >> 1) + step) & 3) + (head & 1)


def one_hot(mask):
    return jnp.where(mask, 1.0, 0.0).astype(bf16)


def own_part(pos_ref, lat_ref, out_ref):
    rows, tokens, width = out_ref.shape[0], lat_ref.shape[0], lat_ref.shape[1]
    row, col = iota((rows, tokens), 0), iota((rows, tokens), 1)
    want = (row >> 2) * BLOCK + part_of(pos_ref[1]) * PART + (row & 3)
    for u in (0, 1):
        lines = dot(one_hot(col == want + u * LINES), lat_ref[...], 1, 0)
        out_ref[:, u * width : (u + 1) * width] = lines.astype(bf16)


def choose(picks_ref, hit_ref, info_ref, ask_ref, *, per_owner):
    picks, queries = picks_ref.shape
    blocks = hit_ref.shape[0]
    block = iota((blocks, queries), 0)
    hit = jnp.zeros((blocks, queries), jnp.bool_)
    for k in range(picks):
        hit = jnp.logical_or(hit, picks_ref[k : k + 1, :] == block)
    hit = one_hot(hit)
    hit_ref[...] = hit
    count = dot(jnp.ones((8, queries), bf16), hit, 1, 1)
    chosen = jnp.where(count > 0.5, 1.0, 0.0)
    lo, hi = iota((blocks, blocks), 0), iota((blocks, blocks), 1)
    same = jnp.logical_and(lo < hi, lo >= by20(hi[:1]) * per_owner)
    rank = dot(chosen.astype(bf16), one_hot(same), 1, 0)
    info_ref[0:8, :] = chosen
    info_ref[8:16, :] = rank
    chosen, rank = chosen[:1], rank[:1]
    rows = ask_ref.shape[0]
    row, col = iota((rows, blocks), 0), iota((1, blocks), 1)
    key = jnp.where(chosen > 0.5, by20(col) * CAP + rank.astype(jnp.int32), -1)
    local_id = (col - by20(col) * per_owner).astype(f32)
    ask = jnp.sum(jnp.where((row >> 2) == key, local_id, 0.0), axis=1, keepdims=True)
    ask_ref[...] = jnp.broadcast_to(ask, ask_ref.shape).astype(bf16)


def fetch(ask_ref, own_ref, out_ref):
    rows, lines = out_ref.shape[0], own_ref.shape[0]
    row, col = iota((rows, lines), 0), iota((rows, lines), 1)
    want = ask_ref[:, :1].astype(f32).astype(jnp.int32) * LINES + (row & 3)
    out_ref[...] = dot(one_hot(col == want), own_ref[...], 1, 0).astype(bf16)


def arrange(
    pos_ref, hit_ref, info_ref, ask_ref, bias_ref, rest_ref, send_ref, back_ref, sum_ref, place_ref,
    *, first, per_dest,
):
    blocks, queries = hit_ref.shape
    rows, slots = send_ref.shape
    head = pos_ref[1]
    chosen8 = info_ref[0:8, :]
    chosen = chosen8[:1]
    rank = info_ref[8:9, :]
    lo, hi = iota((blocks, blocks), 0), iota((blocks, blocks), 1)
    order = dot(chosen8.astype(bf16), one_hot(lo < hi), 1, 0)[:1]
    row = iota((rows, blocks), 0)
    slot = (row >> 2).astype(f32)
    here = jnp.where(jnp.logical_and(order == slot, chosen > 0.5), 1.0, 0.0)
    block_id = jnp.sum(here * iota((rows, blocks), 1).astype(f32), axis=1, keepdims=True)
    block_rank = jnp.sum(here * rank, axis=1, keepdims=True)
    block_id = block_id.astype(jnp.int32)
    block_rank = block_rank.astype(jnp.int32)
    picked = dot(here.astype(bf16), hit_ref[...], 1, 0)
    query_pos = first + pos_ref[0] * queries + iota((rows, queries), 1)
    base = block_id * BLOCK + (iota((rows, queries), 0) & 3) - query_pos
    for i, step in enumerate((0, -1, 1, 2)):
        out_ref = rest_ref if i else bias_ref
        for u in (0, 1):
            offset = near(head, step) * PART + u * LINES
            allowed = jnp.logical_and(picked > 0.5, base + offset <= 0)
            at = (2 * max(i - 1, 0) + u) * rows
            out_ref[at : at + rows, :] = jnp.where(allowed, 0.0, NEG)
    row = iota(send_ref.shape, 0)
    col = iota(send_ref.shape, 1)
    send = one_hot(col == (by20(block_id) * CAP + block_rank) * LINES + (row & 3))
    send_ref[...] = send
    unit = one_hot(iota((rows, rows), 0) == iota((rows, rows), 1))
    back_ref[...] = dot(send, unit, 0, 0).astype(bf16)
    ids = dot(one_hot(iota((8, 128), 1) == 0), ask_ref[...], 1, 1)[:1].astype(jnp.int32)
    row = iota(sum_ref.shape, 0)
    col = iota(sum_ref.shape, 1)
    e = part_of(head)
    dest = row >> 3
    start = ((per_dest * dest - e + 7) >> 3) + ((row >> 2) & 1)
    inside = 8 * start + e < per_dest * (dest + 1)
    match = jnp.logical_and(ids == start, (row & 3) == (col & 3))
    sum_ref[...] = one_hot(jnp.logical_and(match, inside))
    outs = place_ref.shape[0] // 2
    row = iota((outs, place_ref.shape[1]), 0)
    col = iota((outs, place_ref.shape[1]), 1)
    e = part_of(col >> 3)
    start = ((per_dest * head - e + 7) >> 3) + ((col >> 2) & 1)
    match = jnp.logical_and(8 * start + e == per_dest * head + (row >> 3), (row & 3) == (col & 3))
    for u in (0, 1):
        mine = jnp.logical_and(match, ((row >> 2) & 1) == u)
        place_ref[u * outs : (u + 1) * outs, :] = one_hot(mine)


def multiply(a_ref, b_ref, out_ref):
    out_ref[...] = dot(a_ref[...], b_ref[...], 1, 0).astype(out_ref.dtype)


def score_piece(keys, bias, qs_ref, gs_ref, e_ref, d_ref, at):
    tokens, cols = keys.shape[0], qs_ref.shape[0]
    wide = jnp.concatenate([bias] * (cols // bias.shape[1]), axis=1)
    s = dot(keys, qs_ref[...], 1, 1) * score_scale + wide
    d = dot(keys[:, :LAT], gs_ref[...], 1, 1)
    top = jnp.max(s, axis=0, keepdims=True)
    e = jnp.exp(s - top)
    e_ref[at : at + tokens, :] = e
    d_ref[at : at + tokens, :] = d
    return top, jnp.sum(e, axis=0, keepdims=True), jnp.sum(e * d, axis=0, keepdims=True)


def unpack(piece_ref, k_ref, at):
    lines, width = piece_ref.shape[0], k_ref.shape[1]
    for u in (0, 1):
        here = slice(at + u * lines, at + (u + 1) * lines)
        k_ref[here, :] = piece_ref[:, u * width : (u + 1) * width]


def score_own(
    own_ref, q_ref, g_ref, qt_ref, gt_ref, bias_ref, e_ref, d_ref, stat_ref, k_ref, qs_ref, gs_ref
):
    width = k_ref.shape[1]
    queries = q_ref.shape[0]
    heads = g_ref.shape[1] // LAT
    unpack(own_ref, k_ref, 0)
    for c, (x_ref, y_ref) in enumerate(((q_ref, g_ref), (qt_ref, gt_ref))):
        for h in range(heads):
            at = (c * heads + h) * queries
            qs_ref[at : at + queries, :] = x_ref[:, h * width : (h + 1) * width]
            gs_ref[at : at + queries, :] = y_ref[:, h * LAT : (h + 1) * LAT]
    found = score_piece(k_ref[...], bias_ref[...], qs_ref, gs_ref, e_ref, d_ref, 0)
    for i in range(3):
        stat_ref[i : i + 1, :] = found[i]
    stat_ref[3:8, :] = jnp.zeros((5, stat_ref.shape[1]), f32)


def score_rest(
    below_ref, above_ref, far_ref, qs_ref, gs_ref, bias_hbm, first_ref,
    e_ref, d_ref, stat_ref, tops_ref, k_ref, bias_ref, sem,
):
    copy = pltpu.make_async_copy(bias_hbm, bias_ref, sem)
    copy.start()
    size = 2 * below_ref.shape[0]
    pieces = (below_ref, above_ref, far_ref)
    for i, piece_ref in enumerate(pieces):
        unpack(piece_ref, k_ref, i * size)
    copy.wait()
    found = [tuple(first_ref[i : i + 1, :] for i in range(3))]
    for i in range(len(pieces)):
        at = slice(i * size, (i + 1) * size)
        found.append(
            score_piece(k_ref[at, :], bias_ref[at, :], qs_ref, gs_ref, e_ref, d_ref, i * size)
        )
    top = functools.reduce(jnp.maximum, [f[0] for f in found])
    weights = [jnp.exp(f[0] - top) for f in found]
    stat_ref[0:1, :] = top
    stat_ref[1:2, :] = sum(f[1] * w for f, w in zip(found, weights))
    stat_ref[2:3, :] = sum(f[2] * w for f, w in zip(found, weights))
    stat_ref[3:8, :] = jnp.zeros((5, stat_ref.shape[1]), f32)
    for i, f in enumerate(found):
        tops_ref[i : i + 1, :] = f[0]
    tops_ref[4:8, :] = jnp.zeros((4, stat_ref.shape[1]), f32)


def key_side(
    e_ref, d_ref, stat_ref, other_ref, tops_ref, qs_ref, gs_ref, *out_refs, first
):
    *outs, ds_ref = out_refs
    cols, width = qs_ref.shape
    mine = stat_ref[...]
    other = other_ref[...]
    other = jnp.concatenate([other[:, cols // 2 :], other[:, : cols // 2]], axis=1)
    top = jnp.maximum(mine[0:1], other[0:1])
    a, b = jnp.exp(mine[0:1] - top), jnp.exp(other[0:1] - top)
    inv = 1.0 / (mine[1:2] * a + other[1:2] * b)
    delta = (mine[2:3] * a + other[2:3] * b) * inv
    lines = outs[0].shape[0]
    size = 2 * lines
    for i, out_ref in enumerate(outs):
        at = slice(i * size, (i + 1) * size)
        scale = jnp.exp(tops_ref[first + i : first + i + 1, :] - top) * inv
        p = e_ref[at, :] * scale
        ds = (p * (d_ref[at, :] - delta)).astype(bf16)
        ds_ref[at, :] = ds
        dk = dot(ds, qs_ref[...], 1, 0) * score_scale
        dv = dot(p.astype(bf16), gs_ref[...], 1, 0)
        both = jnp.concatenate([dk[:, :LAT] + dv, dk[:, LAT:]], axis=1).astype(out_ref.dtype)
        for u in (0, 1):
            out_ref[:, u * width : (u + 1) * width] = both[u * lines : (u + 1) * lines, :]


def query_side(ds_ref, rest_ref, k_ref, rest_k_ref, mine_ref, other_ref):
    rows, width = mine_ref.shape[0], k_ref.shape[1]
    for i, out_ref in enumerate((mine_ref, other_ref)):
        for u in (0, 1):
            at = slice((2 * i + u) * rows, (2 * i + u + 1) * rows)
            part = dot(ds_ref[:, at], k_ref[...], 0, 0)
            part = part + dot(rest_ref[:, at], rest_k_ref[...], 0, 0)
            out_ref[:, u * width : (u + 1) * width] = part


def query_sum(mine_ref, got_ref, dq_ref):
    queries = dq_ref.shape[0]
    heads, line = mine_ref.shape[0] // queries, mine_ref.shape[1]
    width = line // 2
    for h in range(heads):
        at = slice(h * queries, (h + 1) * queries)
        total = ((mine_ref[at, :] + got_ref[at, :]) * score_scale).astype(bf16)
        dq_ref[:, h * width : (h + 1) * width] = total[:, :width]
        h2 = h + heads
        dq_ref[:, h2 * width : (h2 + 1) * width] = total[:, width:]


def outgoing(back_ref, own_ref, up_ref, down_ref, far_ref, out_ref):
    total = own_ref[...] + up_ref[...].astype(f32)
    total = total + down_ref[...].astype(f32) + far_ref[...].astype(f32)
    out_ref[...] = dot(back_ref[...], total.astype(bf16), 1, 0).astype(bf16)


def place(place_ref, in_ref, out_ref):
    outs, width = out_ref.shape
    first = dot(place_ref[:outs, :], in_ref[:, :width], 1, 0)
    out_ref[...] = first + dot(place_ref[outs:, :], in_ref[:, width:], 1, 0)


def local(latent, query, grad_out, picks):
    n_ctx = lax.axis_size("ctx")
    n_head = lax.axis_size("head")
    ctx_rows, width = latent.shape
    queries = query.shape[0]
    per_owner = ctx_rows // BLOCK
    blocks = per_owner * n_ctx
    line = 2 * width
    pool_lines = POOL * LINES
    slots = n_ctx * CAP * LINES
    piece_rows = 2 * pool_lines
    outs = ctx_rows // n_head
    pos = jnp.stack([lax.axis_index("ctx"), lax.axis_index("head")]).astype(jnp.int32)
    first = (ctx_rows - queries) * n_ctx
    shape = jax.ShapeDtypeStruct
    up = [(i, (i + 2) % n_head) for i in range(n_head)]
    down = [(i, (i - 2) % n_head) for i in range(n_head)]
    across = [(i, (i + 4 - 8 * (i & 1)) % n_head) for i in range(n_head)]
    twin = [(i, i ^ 1) for i in range(n_head)]

    def swap(x, axis):
        n = lax.axis_size(axis)
        x3 = x.reshape(n, -1, x.shape[1])
        return lax.all_to_all(x3, axis, split_axis=0, concat_axis=0, tiled=True).reshape(x.shape)

    hit, info, ask = call(
        functools.partial(choose, per_owner=per_owner),
        (shape((blocks, queries), bf16), shape((16, blocks), f32), shape((slots, 128), bf16)),
        picks.T,
    )
    own = call(own_part, shape((per_owner * LINES, line), bf16), pos, latent, flops=10**9, traffic=10**6)
    asked = swap(ask, "ctx")
    lines_out = call(fetch, shape((slots, line), bf16), asked, own)
    bias, rest_bias, send, back, sums, places = call(
        functools.partial(arrange, first=first, per_dest=outs // PART),
        (
            shape((piece_rows, queries), f32),
            shape((3 * piece_rows, queries), f32),
            shape((pool_lines, slots), bf16),
            shape((slots, pool_lines), bf16),
            shape((n_head * CAP * LINES, slots), bf16),
            shape((2 * outs, n_head * CAP * LINES), bf16),
        ),
        pos,
        hit,
        info,
        asked,
        flops=3 * 10**9,
        traffic=3 * 10**6,
    )
    query, grad_out, bias = lax.optimization_barrier((query, grad_out, bias))
    twin_query = lax.ppermute(query, "head", twin)
    twin_grad = lax.ppermute(grad_out, "head", twin)
    lines_in = swap(lines_out, "ctx")
    mine = call(multiply, shape((pool_lines, line), bf16), send, lines_in)
    from_below = lax.ppermute(mine, "head", up)
    from_above = lax.ppermute(mine, "head", down)
    from_far = lax.ppermute(mine, "head", across)
    rows = queries * (grad_out.shape[1] // LAT)
    cols = 2 * rows

    def arrays(n):
        return shape((n * piece_rows, cols), f32), shape((n * piece_rows, cols), f32)

    row_stats = shape((8, cols), f32)
    scores, prob_grad, first_stats, keys, query_rows, grad_rows = call(
        score_own,
        (
            *arrays(1),
            row_stats,
            shape((piece_rows, width), bf16),
            shape((cols, width), bf16),
            shape((cols, LAT), bf16),
        ),
        mine,
        query,
        grad_out,
        twin_query,
        twin_grad,
        bias,
        flops=10**9,
        traffic=10**6,
        mib=20,
    )
    rest_scores, rest_prob_grad, stats, tops, rest_keys = call(
        score_rest,
        (*arrays(3), row_stats, row_stats, shape((3 * piece_rows, width), bf16)),
        from_below,
        from_above,
        from_far,
        query_rows,
        grad_rows,
        rest_bias,
        first_stats,
        scratch=(pltpu.VMEM((3 * piece_rows, queries), f32), pltpu.SemaphoreType.DMA(())),
        flops=3 * 10**9,
        traffic=10**6,
        mib=20,
        hbm=(5,),
    )
    twin_stats = lax.ppermute(stats, "head", twin)
    piece = shape((pool_lines, line), bf16)
    to_down, to_up, to_far, rest_score_grad = call(
        functools.partial(key_side, first=1),
        (piece, piece, piece, shape((3 * piece_rows, cols), bf16)),
        rest_scores,
        rest_prob_grad,
        stats,
        twin_stats,
        tops,
        query_rows,
        grad_rows,
        flops=3 * 10**9,
        traffic=10**6,
        mib=20,
    )
    sum_far = lax.ppermute(to_far, "head", across)
    sum_up = lax.ppermute(to_up, "head", up)
    sum_down = lax.ppermute(to_down, "head", down)
    to_own, score_grad = call(
        functools.partial(key_side, first=0),
        (shape((pool_lines, line), f32), shape((piece_rows, cols), bf16)),
        scores,
        prob_grad,
        stats,
        twin_stats,
        tops,
        query_rows,
        grad_rows,
        flops=10**9,
        traffic=10**6,
        mib=20,
    )
    half_grad = shape((rows // 2, line), f32)
    query_mine, query_other = call(
        query_side,
        (half_grad, half_grad),
        score_grad,
        rest_score_grad,
        keys,
        rest_keys,
        flops=3 * 10**9,
        traffic=10**7,
    )
    query_got = lax.ppermute(query_other, "head", twin)
    query_grad = call(query_sum, shape(query.shape, bf16), query_mine, query_got)
    outbox = call(outgoing, shape((slots, line), bf16), back, to_own, sum_up, sum_down, sum_far)
    inbox = swap(outbox, "ctx")
    totals = call(multiply, shape((n_head * CAP * LINES, line), bf16), sums, inbox)
    spread = swap(totals, "head")
    grad_latent = call(place, shape((outs, width), f32), places, spread)
    return (query_grad, grad_latent)


def solution(mesh):
    return jax.shard_map(
        local,
        mesh=mesh,
        in_specs=(P("ctx", None), P("ctx", "head"), P("ctx", "head"), P("ctx", None)),
        out_specs=(P("ctx", "head"), P(("ctx", "head"), None)),
        check_vma=False,
    )
```

```python
import functools

import jax
import jax.numpy as jnp
from jax import lax
from jax.experimental import pallas as pl
from jax.experimental.pallas import tpu as pltpu
from jax.sharding import PartitionSpec as P

LAT = 512
BLOCK = 64
POOL = 36
CAP = 2
NEG = -1e30

score_scale = 192.0 ** (-0.5)
bf16 = jnp.bfloat16
f32 = jnp.float32


def iota(shape, dim):
    return lax.broadcasted_iota(jnp.int32, shape, dim)


def by20(x):
    return (x * 3277) >> 16


def dot(a, b, ca, cb):
    return lax.dot_general(a, b, (((ca,), (cb,)), ((), ())), preferred_element_type=f32)


def call(body, out_shape, *args, scratch=(), flops=0, traffic=0, mib=16, hbm=()):
    vmem = pl.BlockSpec(memory_space=pltpu.VMEM)
    smem = pl.BlockSpec(memory_space=pltpu.SMEM)
    specs = [smem if a.dtype == jnp.int32 and a.ndim == 1 else vmem for a in args]
    for i in hbm:
        specs[i] = pl.BlockSpec(memory_space=pl.ANY)
    return pl.pallas_call(
        body,
        out_shape=out_shape,
        in_specs=specs,
        out_specs=jax.tree.map(lambda _: vmem, out_shape),
        scratch_shapes=list(scratch),
        compiler_params=pltpu.CompilerParams(vmem_limit_bytes=mib * 1024 * 1024),
        cost_estimate=pl.CostEstimate(flops=flops, bytes_accessed=traffic, transcendentals=0),
    )(*args)


PART = 8
LINES = 4


def part_of(head):
    return head & 7


def near(head, step):
    return 2 * (((head >> 1) + step) & 3) + (head & 1)


def one_hot(mask):
    return jnp.where(mask, 1.0, 0.0).astype(bf16)


def own_part(pos_ref, lat_ref, out_ref):
    rows, tokens, width = out_ref.shape[0], lat_ref.shape[0], lat_ref.shape[1]
    row, col = iota((rows, tokens), 0), iota((rows, tokens), 1)
    want = (row >> 2) * BLOCK + part_of(pos_ref[1]) * PART + (row & 3)
    for u in (0, 1):
        lines = dot(one_hot(col == want + u * LINES), lat_ref[...], 1, 0)
        out_ref[:, u * width : (u + 1) * width] = lines.astype(bf16)


def hits(picks_ref, blocks):
    picks, queries = picks_ref.shape
    block = iota((blocks, queries), 0)
    hit = jnp.zeros((blocks, queries), jnp.bool_)
    for k in range(picks):
        hit = jnp.logical_or(hit, picks_ref[k : k + 1, :] == block)
    return one_hot(hit)


def choose(picks_ref, hit_ref, ask_ref, *, per_owner):
    blocks, queries = hit_ref.shape
    hit = hits(picks_ref, blocks)
    hit_ref[...] = hit
    count = dot(hit, jnp.ones((queries, 128), bf16), 1, 0)
    row, lane = iota((blocks, 128), 0), iota((blocks, 128), 1)
    owner = by20(row)
    placed = one_hot(jnp.logical_and(count > 0.5, lane == row - owner * per_owner))
    owners = ask_ref.shape[0]
    member = one_hot(by20(iota((owners, blocks), 1)) == iota((owners, blocks), 0))
    table = dot(member, placed, 1, 0)
    before = one_hot(iota((128, 128), 0) < iota((128, 128), 1))
    rank = dot(table.astype(bf16), before, 1, 0)
    lane = iota((owners, 128), 1).astype(f32)
    ids = []
    for k in range(CAP):
        here = jnp.logical_and(table > 0.5, rank == k)
        ids.append(jnp.sum(jnp.where(here, lane, 0.0), axis=1, keepdims=True))
    line = iota(ask_ref.shape, 1)
    ask = jnp.where(line < LINES, ids[0][:, :, None], ids[1][:, :, None])
    ask_ref[...] = ask.astype(bf16)


def fetch(ask_ref, own_ref, out_ref):
    rows, lines = out_ref.shape[0], own_ref.shape[0]
    row, col = iota((rows, lines), 0), iota((rows, lines), 1)
    want = ask_ref[:, :1].astype(f32).astype(jnp.int32) * LINES + (row & 3)
    out_ref[...] = dot(one_hot(col == want), own_ref[...], 1, 0).astype(bf16)


def arrange(
    pos_ref, hit_ref, ask_ref, bias_ref, near_ref, far_ref, send_ref, back_ref, sum_ref, place_ref,
    *, first, per_dest, per_owner,
):
    blocks, queries = hit_ref.shape
    rows, slots = send_ref.shape
    head = pos_ref[1]
    count = dot(jnp.ones((8, queries), bf16), hit_ref[...], 1, 1)
    chosen8 = one_hot(count > 0.5)
    chosen = count[:1]
    lo, hi = iota((blocks, blocks), 0), iota((blocks, blocks), 1)
    order = dot(chosen8, one_hot(lo < hi), 1, 0)[:1]
    same = jnp.logical_and(lo < hi, lo >= by20(hi[:1]) * per_owner)
    rank = dot(chosen8, one_hot(same), 1, 0)[:1]
    row = iota((rows, blocks), 0)
    slot = (row >> 2).astype(f32)
    here = jnp.where(jnp.logical_and(order == slot, chosen > 0.5), 1.0, 0.0)
    block_id = jnp.sum(here * iota((rows, blocks), 1).astype(f32), axis=1, keepdims=True)
    block_rank = jnp.sum(here * rank, axis=1, keepdims=True)
    block_id = block_id.astype(jnp.int32)
    block_rank = block_rank.astype(jnp.int32)
    picked = dot(here.astype(bf16), hit_ref[...], 1, 0)
    query_pos = first + pos_ref[0] * queries + iota((rows, queries), 1)
    base = block_id * BLOCK + (iota((rows, queries), 0) & 3) - query_pos
    for i, step in enumerate((0, -1, 1, 2)):
        out_ref = (bias_ref, near_ref, near_ref, far_ref)[i]
        for u in (0, 1):
            offset = near(head, step) * PART + u * LINES
            allowed = jnp.logical_and(picked > 0.5, base + offset <= 0)
            at = (2 * (i == 2) + u) * rows
            out_ref[at : at + rows, :] = jnp.where(allowed, 0.0, NEG)
    row = iota(send_ref.shape, 0)
    col = iota(send_ref.shape, 1)
    send = one_hot(col == (by20(block_id) * CAP + block_rank) * LINES + (row & 3))
    send_ref[...] = send
    unit = one_hot(iota((rows, rows), 0) == iota((rows, rows), 1))
    back_ref[...] = dot(send, unit, 0, 0).astype(bf16)
    ids = dot(one_hot(iota((8, 128), 1) == 0), ask_ref[...], 1, 1)[:1].astype(jnp.int32)
    row = iota(sum_ref.shape, 0)
    col = iota(sum_ref.shape, 1)
    e = part_of(head)
    dest = row >> 3
    start = ((per_dest * dest - e + 7) >> 3) + ((row >> 2) & 1)
    inside = 8 * start + e < per_dest * (dest + 1)
    match = jnp.logical_and(ids == start, (row & 3) == (col & 3))
    sum_ref[...] = one_hot(jnp.logical_and(match, inside))
    outs = place_ref.shape[0] // 2
    row = iota((outs, place_ref.shape[1]), 0)
    col = iota((outs, place_ref.shape[1]), 1)
    e = part_of(col >> 3)
    start = ((per_dest * head - e + 7) >> 3) + ((col >> 2) & 1)
    match = jnp.logical_and(8 * start + e == per_dest * head + (row >> 3), (row & 3) == (col & 3))
    for u in (0, 1):
        mine = jnp.logical_and(match, ((row >> 2) & 1) == u)
        place_ref[u * outs : (u + 1) * outs, :] = one_hot(mine)


def multiply(a_ref, b_ref, out_ref):
    out_ref[...] = dot(a_ref[...], b_ref[...], 1, 0).astype(out_ref.dtype)


def score_piece(keys, bias, qs_ref, gs_ref, e_ref, d_ref, at):
    tokens, cols = keys.shape[0], qs_ref.shape[0]
    wide = jnp.concatenate([bias] * (cols // bias.shape[1]), axis=1)
    s = dot(keys, qs_ref[...], 1, 1) * score_scale + wide
    d = dot(keys[:, :LAT], gs_ref[...], 1, 1)
    top = jnp.max(s, axis=0, keepdims=True)
    e = jnp.exp(s - top)
    e_ref[at : at + tokens, :] = e
    d_ref[at : at + tokens, :] = d
    return top, jnp.sum(e, axis=0, keepdims=True), jnp.sum(e * d, axis=0, keepdims=True)


def unpack(piece_ref, k_ref, at):
    lines, width = piece_ref.shape[0], k_ref.shape[1]
    for u in (0, 1):
        here = slice(at + u * lines, at + (u + 1) * lines)
        k_ref[here, :] = piece_ref[:, u * width : (u + 1) * width]


def score_own(
    own_ref, q_ref, g_ref, qt_ref, gt_ref, bias_ref, e_ref, d_ref, stat_ref, k_ref, qs_ref, gs_ref
):
    width = k_ref.shape[1]
    queries = q_ref.shape[0]
    heads = g_ref.shape[1] // LAT
    unpack(own_ref, k_ref, 0)
    for c, (x_ref, y_ref) in enumerate(((q_ref, g_ref), (qt_ref, gt_ref))):
        for h in range(heads):
            at = (c * heads + h) * queries
            qs_ref[at : at + queries, :] = x_ref[:, h * width : (h + 1) * width]
            gs_ref[at : at + queries, :] = y_ref[:, h * LAT : (h + 1) * LAT]
    found = score_piece(k_ref[...], bias_ref[...], qs_ref, gs_ref, e_ref, d_ref, 0)
    for i in range(3):
        stat_ref[i : i + 1, :] = found[i]
    stat_ref[3:8, :] = jnp.zeros((5, stat_ref.shape[1]), f32)


def score_near(
    below_ref, above_ref, qs_ref, gs_ref, bias_hbm, e_ref, d_ref, stat_ref, k_ref, bias_ref, sem
):
    copy = pltpu.make_async_copy(bias_hbm, bias_ref, sem)
    copy.start()
    size = 2 * below_ref.shape[0]
    unpack(below_ref, k_ref, 0)
    unpack(above_ref, k_ref, size)
    copy.wait()
    for i in (0, 1):
        at = slice(i * size, (i + 1) * size)
        found = score_piece(k_ref[at, :], bias_ref[at, :], qs_ref, gs_ref, e_ref, d_ref, i * size)
        for j in range(3):
            stat_ref[3 * i + j : 3 * i + j + 1, :] = found[j]
    stat_ref[6:8, :] = jnp.zeros((2, stat_ref.shape[1]), f32)


def score_far(
    far_ref, qs_ref, gs_ref, bias_hbm, own_ref, near_ref,
    e_ref, d_ref, stat_ref, tops_ref, k_ref, bias_ref, sem,
):
    copy = pltpu.make_async_copy(bias_hbm, bias_ref, sem)
    copy.start()
    unpack(far_ref, k_ref, 0)
    copy.wait()
    found = [tuple(own_ref[j : j + 1, :] for j in range(3))]
    for i in (0, 1):
        found.append(tuple(near_ref[3 * i + j : 3 * i + j + 1, :] for j in range(3)))
    found.append(score_piece(k_ref[...], bias_ref[...], qs_ref, gs_ref, e_ref, d_ref, 0))
    top = functools.reduce(jnp.maximum, [f[0] for f in found])
    weights = [jnp.exp(f[0] - top) for f in found]
    stat_ref[0:1, :] = top
    stat_ref[1:2, :] = sum(f[1] * w for f, w in zip(found, weights))
    stat_ref[2:3, :] = sum(f[2] * w for f, w in zip(found, weights))
    stat_ref[3:8, :] = jnp.zeros((5, stat_ref.shape[1]), f32)
    for i, f in enumerate(found):
        tops_ref[i : i + 1, :] = f[0]
    tops_ref[4:8, :] = jnp.zeros((4, stat_ref.shape[1]), f32)


def key_side(
    e_ref, d_ref, stat_ref, other_ref, tops_ref, qs_ref, gs_ref, *out_refs, first
):
    *outs, ds_ref = out_refs
    cols, width = qs_ref.shape
    mine = stat_ref[...]
    other = other_ref[...]
    other = jnp.concatenate([other[:, cols // 2 :], other[:, : cols // 2]], axis=1)
    top = jnp.maximum(mine[0:1], other[0:1])
    a, b = jnp.exp(mine[0:1] - top), jnp.exp(other[0:1] - top)
    inv = 1.0 / (mine[1:2] * a + other[1:2] * b)
    delta = (mine[2:3] * a + other[2:3] * b) * inv
    lines = outs[0].shape[0]
    size = 2 * lines
    for i, out_ref in enumerate(outs):
        at = slice(i * size, (i + 1) * size)
        scale = jnp.exp(tops_ref[first + i : first + i + 1, :] - top) * inv
        p = e_ref[at, :] * scale
        ds = (p * (d_ref[at, :] - delta)).astype(bf16)
        ds_ref[at, :] = ds
        dk = dot(ds, qs_ref[...], 1, 0) * score_scale
        dv = dot(p.astype(bf16), gs_ref[...], 1, 0)
        both = jnp.concatenate([dk[:, :LAT] + dv, dk[:, LAT:]], axis=1).astype(out_ref.dtype)
        for u in (0, 1):
            out_ref[:, u * width : (u + 1) * width] = both[u * lines : (u + 1) * lines, :]


def query_side(ds0_ref, ds1_ref, ds2_ref, k0_ref, k1_ref, k2_ref, mine_ref, other_ref):
    rows, width = mine_ref.shape[0], k0_ref.shape[1]
    for i, out_ref in enumerate((mine_ref, other_ref)):
        for u in (0, 1):
            at = slice((2 * i + u) * rows, (2 * i + u + 1) * rows)
            part = dot(ds0_ref[:, at], k0_ref[...], 0, 0)
            part = part + dot(ds1_ref[:, at], k1_ref[...], 0, 0)
            part = part + dot(ds2_ref[:, at], k2_ref[...], 0, 0)
            out_ref[:, u * width : (u + 1) * width] = part


def join(pos_ref, up_ref, down_ref, got_ref, up_out_ref, down_out_ref):
    core = (pos_ref[1] & 1).astype(f32)
    got = got_ref[...].astype(f32)
    up_out_ref[...] = (up_ref[...] + got * (1.0 - core)).astype(bf16)
    down_out_ref[...] = (down_ref[...] + got * core).astype(bf16)


def query_sum(mine_ref, got_ref, dq_ref):
    queries = dq_ref.shape[0]
    heads, line = mine_ref.shape[0] // queries, mine_ref.shape[1]
    width = line // 2
    for h in range(heads):
        at = slice(h * queries, (h + 1) * queries)
        total = ((mine_ref[at, :] + got_ref[at, :]) * score_scale).astype(bf16)
        dq_ref[:, h * width : (h + 1) * width] = total[:, :width]
        h2 = h + heads
        dq_ref[:, h2 * width : (h2 + 1) * width] = total[:, width:]


def outgoing(back_ref, own_ref, up_ref, down_ref, out_ref):
    total = own_ref[...] + up_ref[...].astype(f32) + down_ref[...].astype(f32)
    out_ref[...] = dot(back_ref[...], total.astype(bf16), 1, 0).astype(bf16)


def place(place_ref, in_ref, out_ref):
    outs, width = out_ref.shape
    first = dot(place_ref[:outs, :], in_ref[:, :width], 1, 0)
    out_ref[...] = first + dot(place_ref[outs:, :], in_ref[:, width:], 1, 0)


def local(latent, query, grad_out, picks):
    n_ctx = lax.axis_size("ctx")
    n_head = lax.axis_size("head")
    ctx_rows, width = latent.shape
    queries = query.shape[0]
    per_owner = ctx_rows // BLOCK
    blocks = per_owner * n_ctx
    line = 2 * width
    pool_lines = POOL * LINES
    slots = n_ctx * CAP * LINES
    piece_rows = 2 * pool_lines
    outs = ctx_rows // n_head
    pos = jnp.stack([lax.axis_index("ctx"), lax.axis_index("head")]).astype(jnp.int32)
    first = (ctx_rows - queries) * n_ctx
    shape = jax.ShapeDtypeStruct
    up = [(i, (i + 2) % n_head) for i in range(n_head)]
    down = [(i, (i - 2) % n_head) for i in range(n_head)]
    relay = [(i, (i + 2 - 4 * (i & 1)) % n_head) for i in range(n_head)]
    twin = [(i, i ^ 1) for i in range(n_head)]

    def swap(x, axis):
        n = lax.axis_size(axis)
        x3 = x.reshape(n, -1, x.shape[1])
        return lax.all_to_all(x3, axis, split_axis=0, concat_axis=0, tiled=True).reshape(x.shape)

    hit, ask = call(
        functools.partial(choose, per_owner=per_owner),
        (shape((blocks, queries), bf16), shape((n_ctx, CAP * LINES, 128), bf16)),
        picks.T,
    )
    ask = ask.reshape(slots, 128)
    own = call(own_part, shape((per_owner * LINES, line), bf16), pos, latent, flops=10**9, traffic=10**6)
    asked = swap(ask, "ctx")
    lines_out = call(fetch, shape((slots, line), bf16), asked, own)
    bias, near_bias, far_bias, send, back, sums, places = call(
        functools.partial(arrange, first=first, per_dest=outs // PART, per_owner=per_owner),
        (
            shape((piece_rows, queries), f32),
            shape((2 * piece_rows, queries), f32),
            shape((piece_rows, queries), f32),
            shape((pool_lines, slots), bf16),
            shape((slots, pool_lines), bf16),
            shape((n_head * CAP * LINES, slots), bf16),
            shape((2 * outs, n_head * CAP * LINES), bf16),
        ),
        pos,
        hit,
        asked,
        flops=3 * 10**9,
        traffic=3 * 10**6,
    )
    query, grad_out, bias = lax.optimization_barrier((query, grad_out, bias))
    twin_query = lax.ppermute(query, "head", twin)
    twin_grad = lax.ppermute(grad_out, "head", twin)
    lines_in = swap(lines_out, "ctx")
    mine = call(multiply, shape((pool_lines, line), bf16), send, lines_in)
    from_below = lax.ppermute(mine, "head", up)
    from_above = lax.ppermute(mine, "head", down)
    onward = jnp.where(pos[1] & 1 == 0, from_below, from_above)
    from_far = lax.ppermute(onward, "head", relay)
    rows = queries * (grad_out.shape[1] // LAT)
    cols = 2 * rows

    def arrays(n):
        return shape((n * piece_rows, cols), f32), shape((n * piece_rows, cols), f32)

    row_stats = shape((8, cols), f32)
    scores, prob_grad, first_stats, keys, query_rows, grad_rows = call(
        score_own,
        (
            *arrays(1),
            row_stats,
            shape((piece_rows, width), bf16),
            shape((cols, width), bf16),
            shape((cols, LAT), bf16),
        ),
        mine,
        query,
        grad_out,
        twin_query,
        twin_grad,
        bias,
        flops=10**9,
        traffic=10**6,
        mib=20,
    )
    near_scores, near_prob_grad, near_stats, near_keys = call(
        score_near,
        (*arrays(2), row_stats, shape((2 * piece_rows, width), bf16)),
        from_below,
        from_above,
        query_rows,
        grad_rows,
        near_bias,
        scratch=(pltpu.VMEM((2 * piece_rows, queries), f32), pltpu.SemaphoreType.DMA(())),
        flops=2 * 10**9,
        traffic=10**6,
        mib=20,
        hbm=(4,),
    )
    far_scores, far_prob_grad, stats, tops, far_keys = call(
        score_far,
        (*arrays(1), row_stats, row_stats, shape((piece_rows, width), bf16)),
        from_far,
        query_rows,
        grad_rows,
        far_bias,
        first_stats,
        near_stats,
        scratch=(pltpu.VMEM((piece_rows, queries), f32), pltpu.SemaphoreType.DMA(())),
        flops=10**9,
        traffic=10**6,
        mib=20,
        hbm=(3,),
    )
    twin_stats = lax.ppermute(stats, "head", twin)

    def key_grad(first, n, dtype, e, d):
        return call(
            functools.partial(key_side, first=first),
            (shape((pool_lines, line), dtype),) * n + (shape((n * piece_rows, cols), bf16),),
            e,
            d,
            stats,
            twin_stats,
            tops,
            query_rows,
            grad_rows,
            flops=n * 10**9,
            traffic=10**6,
            mib=20,
        )

    to_far, far_score_grad = key_grad(3, 1, bf16, far_scores, far_prob_grad)
    got_far = lax.ppermute(to_far, "head", relay)
    to_down, to_up, near_score_grad = key_grad(1, 2, f32, near_scores, near_prob_grad)
    to_own, score_grad = key_grad(0, 1, f32, scores, prob_grad)
    piece = shape((pool_lines, line), bf16)
    to_up, to_down = call(join, (piece, piece), pos, to_up, to_down, got_far)
    sum_up = lax.ppermute(to_up, "head", up)
    sum_down = lax.ppermute(to_down, "head", down)
    half_grad = shape((rows // 2, line), f32)
    query_mine, query_other = call(
        query_side,
        (half_grad, half_grad),
        score_grad,
        near_score_grad,
        far_score_grad,
        keys,
        near_keys,
        far_keys,
        flops=3 * 10**9,
        traffic=10**7,
    )
    query_got = lax.ppermute(query_other, "head", twin)
    query_grad = call(query_sum, shape(query.shape, bf16), query_mine, query_got)
    outbox = call(outgoing, shape((slots, line), bf16), back, to_own, sum_up, sum_down)
    inbox = swap(outbox, "ctx")
    totals = call(multiply, shape((n_head * CAP * LINES, line), bf16), sums, inbox)
    spread = swap(totals, "head")
    grad_latent = call(place, shape((outs, width), f32), places, spread)
    return (query_grad, grad_latent)


def solution(mesh):
    return jax.shard_map(
        local,
        mesh=mesh,
        in_specs=(P("ctx", None), P("ctx", "head"), P("ctx", "head"), P("ctx", None)),
        out_specs=(P("ctx", "head"), P(("ctx", "head"), None)),
        check_vma=False,
    )
```

```python
import functools

import jax
import jax.numpy as jnp
from jax import lax
from jax.experimental import pallas as pl
from jax.experimental.pallas import tpu as pltpu
from jax.sharding import PartitionSpec as P

LAT = 512
BLOCK = 64
POOL = 36
CAP = 2
NEG = -1e30

score_scale = 192.0 ** (-0.5)
bf16 = jnp.bfloat16
f32 = jnp.float32


def iota(shape, dim):
    return lax.broadcasted_iota(jnp.int32, shape, dim)


def by20(x):
    return (x * 3277) >> 16


def dot(a, b, ca, cb):
    return lax.dot_general(a, b, (((ca,), (cb,)), ((), ())), preferred_element_type=f32)


def call(body, out_shape, *args, scratch=(), flops=0, traffic=0, mib=16, hbm=()):
    vmem = pl.BlockSpec(memory_space=pltpu.VMEM)
    smem = pl.BlockSpec(memory_space=pltpu.SMEM)
    specs = [smem if a.dtype == jnp.int32 and a.ndim == 1 else vmem for a in args]
    for i in hbm:
        specs[i] = pl.BlockSpec(memory_space=pl.ANY)
    return pl.pallas_call(
        body,
        out_shape=out_shape,
        in_specs=specs,
        out_specs=jax.tree.map(lambda _: vmem, out_shape),
        scratch_shapes=list(scratch),
        compiler_params=pltpu.CompilerParams(vmem_limit_bytes=mib * 1024 * 1024),
        cost_estimate=pl.CostEstimate(flops=flops, bytes_accessed=traffic, transcendentals=0),
    )(*args)


PART = 8
LINES = 4


def part_of(head):
    return head & 7


def near(head, step):
    return 2 * (((head >> 1) + step) & 3) + (head & 1)


def one_hot(mask):
    return jnp.where(mask, 1.0, 0.0).astype(bf16)


def own_part(pos_ref, lat_ref, out_ref):
    rows, tokens, width = out_ref.shape[0], lat_ref.shape[0], lat_ref.shape[1]
    row, col = iota((rows, tokens), 0), iota((rows, tokens), 1)
    want = (row >> 2) * BLOCK + part_of(pos_ref[1]) * PART + (row & 3)
    for u in (0, 1):
        lines = dot(one_hot(col == want + u * LINES), lat_ref[...], 1, 0)
        out_ref[:, u * width : (u + 1) * width] = lines.astype(bf16)


def hits(picks_ref, blocks):
    picks, queries = picks_ref.shape
    block = iota((blocks, queries), 0)
    least = jnp.full((blocks, queries), blocks, jnp.int32)
    for k in range(picks):
        least = jnp.minimum(least, picks_ref[k : k + 1, :] ^ block)
    return one_hot(least == 0)


def choose(picks_ref, hit_ref, ask_ref, *, per_owner):
    blocks, queries = hit_ref.shape
    hit = hits(picks_ref, blocks)
    hit_ref[...] = hit
    count = dot(hit, jnp.ones((queries, 128), bf16), 1, 0)
    row, lane = iota((blocks, 128), 0), iota((blocks, 128), 1)
    owner = by20(row)
    placed = one_hot(jnp.logical_and(count > 0.5, lane == row - owner * per_owner))
    owners = ask_ref.shape[0]
    member = one_hot(by20(iota((owners, blocks), 1)) == iota((owners, blocks), 0))
    table = dot(member, placed, 1, 0)
    before = one_hot(iota((128, 128), 0) < iota((128, 128), 1))
    rank = dot(table.astype(bf16), before, 1, 0)
    lane = iota((owners, 128), 1).astype(f32)
    ids = []
    for k in range(CAP):
        here = jnp.logical_and(table > 0.5, rank == k)
        ids.append(jnp.sum(jnp.where(here, lane, 0.0), axis=1, keepdims=True))
    line = iota(ask_ref.shape, 1)
    ask = jnp.where(line < LINES, ids[0][:, :, None], ids[1][:, :, None])
    ask_ref[...] = ask.astype(bf16)


def fetch(ask_ref, own_ref, out_ref):
    rows, lines = out_ref.shape[0], own_ref.shape[0]
    row, col = iota((rows, lines), 0), iota((rows, lines), 1)
    want = ask_ref[:, :1].astype(f32).astype(jnp.int32) * LINES + (row & 3)
    out_ref[...] = dot(one_hot(col == want), own_ref[...], 1, 0).astype(bf16)


def arrange(
    pos_ref, hit_ref, ask_ref, bias_ref, near_ref, far_ref, send_ref, back_ref, sum_ref, place_ref,
    *, first, per_dest, per_owner,
):
    blocks, queries = hit_ref.shape
    rows, slots = send_ref.shape
    head = pos_ref[1]
    count = dot(jnp.ones((8, queries), bf16), hit_ref[...], 1, 1)
    chosen8 = one_hot(count > 0.5)
    chosen = count[:1]
    lo, hi = iota((blocks, blocks), 0), iota((blocks, blocks), 1)
    order = dot(chosen8, one_hot(lo < hi), 1, 0)[:1]
    same = jnp.logical_and(lo < hi, lo >= by20(hi[:1]) * per_owner)
    rank = dot(chosen8, one_hot(same), 1, 0)[:1]
    row = iota((rows, blocks), 0)
    slot = (row >> 2).astype(f32)
    here = jnp.where(jnp.logical_and(order == slot, chosen > 0.5), 1.0, 0.0)
    block_id = jnp.sum(here * iota((rows, blocks), 1).astype(f32), axis=1, keepdims=True)
    block_rank = jnp.sum(here * rank, axis=1, keepdims=True)
    block_id = block_id.astype(jnp.int32)
    block_rank = block_rank.astype(jnp.int32)
    picked = dot(here.astype(bf16), hit_ref[...], 1, 0)
    query_pos = first + pos_ref[0] * queries + iota((rows, queries), 1)
    base = block_id * BLOCK + (iota((rows, queries), 0) & 3) - query_pos
    for i, step in enumerate((0, -1, 1, 2)):
        out_ref = (bias_ref, near_ref, near_ref, far_ref)[i]
        for u in (0, 1):
            offset = near(head, step) * PART + u * LINES
            allowed = jnp.logical_and(picked > 0.5, base + offset <= 0)
            at = (2 * (i == 2) + u) * rows
            out_ref[at : at + rows, :] = jnp.where(allowed, 0.0, NEG)
    row = iota(send_ref.shape, 0)
    col = iota(send_ref.shape, 1)
    send = one_hot(col == (by20(block_id) * CAP + block_rank) * LINES + (row & 3))
    send_ref[...] = send
    unit = one_hot(iota((rows, rows), 0) == iota((rows, rows), 1))
    back_ref[...] = dot(send, unit, 0, 0).astype(bf16)
    ids = dot(one_hot(iota((8, 128), 1) == 0), ask_ref[...], 1, 1)[:1].astype(jnp.int32)
    row = iota(sum_ref.shape, 0)
    col = iota(sum_ref.shape, 1)
    e = part_of(head)
    dest = row >> 3
    start = ((per_dest * dest - e + 7) >> 3) + ((row >> 2) & 1)
    inside = 8 * start + e < per_dest * (dest + 1)
    match = jnp.logical_and(ids == start, (row & 3) == (col & 3))
    sum_ref[...] = one_hot(jnp.logical_and(match, inside))
    outs = place_ref.shape[0] // 2
    row = iota((outs, place_ref.shape[1]), 0)
    col = iota((outs, place_ref.shape[1]), 1)
    e = part_of(col >> 3)
    start = ((per_dest * head - e + 7) >> 3) + ((col >> 2) & 1)
    match = jnp.logical_and(8 * start + e == per_dest * head + (row >> 3), (row & 3) == (col & 3))
    for u in (0, 1):
        mine = jnp.logical_and(match, ((row >> 2) & 1) == u)
        place_ref[u * outs : (u + 1) * outs, :] = one_hot(mine)


def multiply(a_ref, b_ref, out_ref):
    out_ref[...] = dot(a_ref[...], b_ref[...], 1, 0).astype(out_ref.dtype)


def score_piece(keys, bias, qs_ref, gs_ref, e_ref, d_ref, at):
    tokens, cols = keys.shape[0], qs_ref.shape[0]
    wide = jnp.concatenate([bias] * (cols // bias.shape[1]), axis=1)
    s = dot(keys, qs_ref[...], 1, 1) * score_scale + wide
    d = dot(keys[:, :LAT], gs_ref[...], 1, 1)
    top = jnp.max(s, axis=0, keepdims=True)
    e = jnp.exp(s - top)
    e_ref[at : at + tokens, :] = e
    d_ref[at : at + tokens, :] = d
    return top, jnp.sum(e, axis=0, keepdims=True), jnp.sum(e * d, axis=0, keepdims=True)


def unpack(piece_ref, k_ref, at):
    lines, width = piece_ref.shape[0], k_ref.shape[1]
    for u in (0, 1):
        here = slice(at + u * lines, at + (u + 1) * lines)
        k_ref[here, :] = piece_ref[:, u * width : (u + 1) * width]


def score_own(
    own_ref, q_ref, g_ref, qt_ref, gt_ref, bias_ref, e_ref, d_ref, stat_ref, k_ref, qs_ref, gs_ref
):
    width = k_ref.shape[1]
    queries = q_ref.shape[0]
    heads = g_ref.shape[1] // LAT
    unpack(own_ref, k_ref, 0)
    for c, (x_ref, y_ref) in enumerate(((q_ref, g_ref), (qt_ref, gt_ref))):
        for h in range(heads):
            at = (c * heads + h) * queries
            qs_ref[at : at + queries, :] = x_ref[:, h * width : (h + 1) * width]
            gs_ref[at : at + queries, :] = y_ref[:, h * LAT : (h + 1) * LAT]
    found = score_piece(k_ref[...], bias_ref[...], qs_ref, gs_ref, e_ref, d_ref, 0)
    for i in range(3):
        stat_ref[i : i + 1, :] = found[i]
    stat_ref[3:8, :] = jnp.zeros((5, stat_ref.shape[1]), f32)


def score_near(
    below_ref, above_ref, qs_ref, gs_ref, bias_hbm, e_ref, d_ref, stat_ref, k_ref, bias_ref, sem
):
    copy = pltpu.make_async_copy(bias_hbm, bias_ref, sem)
    copy.start()
    size = 2 * below_ref.shape[0]
    unpack(below_ref, k_ref, 0)
    unpack(above_ref, k_ref, size)
    copy.wait()
    for i in (0, 1):
        at = slice(i * size, (i + 1) * size)
        found = score_piece(k_ref[at, :], bias_ref[at, :], qs_ref, gs_ref, e_ref, d_ref, i * size)
        for j in range(3):
            stat_ref[3 * i + j : 3 * i + j + 1, :] = found[j]
    stat_ref[6:8, :] = jnp.zeros((2, stat_ref.shape[1]), f32)


def score_far(
    far_ref, qs_ref, gs_ref, bias_hbm, own_ref, near_ref,
    e_ref, d_ref, stat_ref, tops_ref, k_ref, bias_ref, sem,
):
    copy = pltpu.make_async_copy(bias_hbm, bias_ref, sem)
    copy.start()
    unpack(far_ref, k_ref, 0)
    copy.wait()
    found = [tuple(own_ref[j : j + 1, :] for j in range(3))]
    for i in (0, 1):
        found.append(tuple(near_ref[3 * i + j : 3 * i + j + 1, :] for j in range(3)))
    found.append(score_piece(k_ref[...], bias_ref[...], qs_ref, gs_ref, e_ref, d_ref, 0))
    top = functools.reduce(jnp.maximum, [f[0] for f in found])
    weights = [jnp.exp(f[0] - top) for f in found]
    stat_ref[0:1, :] = top
    stat_ref[1:2, :] = sum(f[1] * w for f, w in zip(found, weights))
    stat_ref[2:3, :] = sum(f[2] * w for f, w in zip(found, weights))
    stat_ref[3:8, :] = jnp.zeros((5, stat_ref.shape[1]), f32)
    for i, f in enumerate(found):
        tops_ref[i : i + 1, :] = f[0]
    tops_ref[4:8, :] = jnp.zeros((4, stat_ref.shape[1]), f32)


def key_side(
    e_ref, d_ref, stat_ref, other_ref, tops_ref, qs_ref, gs_ref, *out_refs, first
):
    *outs, ds_ref = out_refs
    cols, width = qs_ref.shape
    mine = stat_ref[...]
    other = other_ref[...]
    other = jnp.concatenate([other[:, cols // 2 :], other[:, : cols // 2]], axis=1)
    top = jnp.maximum(mine[0:1], other[0:1])
    a, b = jnp.exp(mine[0:1] - top), jnp.exp(other[0:1] - top)
    inv = 1.0 / (mine[1:2] * a + other[1:2] * b)
    delta = (mine[2:3] * a + other[2:3] * b) * inv
    lines = outs[0].shape[0]
    size = 2 * lines
    for i, out_ref in enumerate(outs):
        at = slice(i * size, (i + 1) * size)
        scale = jnp.exp(tops_ref[first + i : first + i + 1, :] - top) * inv
        p = e_ref[at, :] * scale
        ds = (p * (d_ref[at, :] - delta)).astype(bf16)
        ds_ref[at, :] = ds
        dk = dot(ds, qs_ref[...], 1, 0) * score_scale
        dv = dot(p.astype(bf16), gs_ref[...], 1, 0)
        both = jnp.concatenate([dk[:, :LAT] + dv, dk[:, LAT:]], axis=1).astype(out_ref.dtype)
        for u in (0, 1):
            out_ref[:, u * width : (u + 1) * width] = both[u * lines : (u + 1) * lines, :]


def query_side(ds0_ref, ds1_ref, ds2_ref, k0_ref, k1_ref, k2_ref, mine_ref, other_ref):
    rows, width = mine_ref.shape[0], k0_ref.shape[1]
    for i, out_ref in enumerate((mine_ref, other_ref)):
        for u in (0, 1):
            at = slice((2 * i + u) * rows, (2 * i + u + 1) * rows)
            part = dot(ds0_ref[:, at], k0_ref[...], 0, 0)
            part = part + dot(ds1_ref[:, at], k1_ref[...], 0, 0)
            part = part + dot(ds2_ref[:, at], k2_ref[...], 0, 0)
            out_ref[:, u * width : (u + 1) * width] = part


def query_sum(mine_ref, got_ref, dq_ref):
    queries = dq_ref.shape[0]
    heads, line = mine_ref.shape[0] // queries, mine_ref.shape[1]
    width = line // 2
    for h in range(heads):
        at = slice(h * queries, (h + 1) * queries)
        total = ((mine_ref[at, :] + got_ref[at, :]) * score_scale).astype(bf16)
        dq_ref[:, h * width : (h + 1) * width] = total[:, :width]
        h2 = h + heads
        dq_ref[:, h2 * width : (h2 + 1) * width] = total[:, width:]


def outgoing(back_ref, own_ref, up_ref, down_ref, far_ref, out_ref):
    total = own_ref[...] + up_ref[...].astype(f32)
    total = total + down_ref[...].astype(f32) + far_ref[...].astype(f32)
    out_ref[...] = dot(back_ref[...], total.astype(bf16), 1, 0).astype(bf16)


def place(place_ref, in_ref, out_ref):
    outs, width = out_ref.shape
    first = dot(place_ref[:outs, :], in_ref[:, :width], 1, 0)
    out_ref[...] = first + dot(place_ref[outs:, :], in_ref[:, width:], 1, 0)


def local(latent, query, grad_out, picks):
    n_ctx = lax.axis_size("ctx")
    n_head = lax.axis_size("head")
    ctx_rows, width = latent.shape
    queries = query.shape[0]
    per_owner = ctx_rows // BLOCK
    blocks = per_owner * n_ctx
    line = 2 * width
    pool_lines = POOL * LINES
    slots = n_ctx * CAP * LINES
    piece_rows = 2 * pool_lines
    outs = ctx_rows // n_head
    pos = jnp.stack([lax.axis_index("ctx"), lax.axis_index("head")]).astype(jnp.int32)
    first = (ctx_rows - queries) * n_ctx
    shape = jax.ShapeDtypeStruct
    up = [(i, (i + 2) % n_head) for i in range(n_head)]
    down = [(i, (i - 2) % n_head) for i in range(n_head)]
    across = [(i, (i + 4 - 8 * (i & 1)) % n_head) for i in range(n_head)]
    relay = [(i, (i + 2 - 4 * (i & 1)) % n_head) for i in range(n_head)]
    twin = [(i, i ^ 1) for i in range(n_head)]

    def swap(x, axis):
        n = lax.axis_size(axis)
        x3 = x.reshape(n, -1, x.shape[1])
        return lax.all_to_all(x3, axis, split_axis=0, concat_axis=0, tiled=True).reshape(x.shape)

    hit, ask = call(
        functools.partial(choose, per_owner=per_owner),
        (shape((blocks, queries), bf16), shape((n_ctx, CAP * LINES, 128), bf16)),
        picks.T,
    )
    ask = ask.reshape(slots, 128)
    own = call(own_part, shape((per_owner * LINES, line), bf16), pos, latent, flops=10**9, traffic=10**6)
    asked = swap(ask, "ctx")
    lines_out = call(fetch, shape((slots, line), bf16), asked, own)
    bias, near_bias, far_bias, send, back, sums, places = call(
        functools.partial(arrange, first=first, per_dest=outs // PART, per_owner=per_owner),
        (
            shape((piece_rows, queries), f32),
            shape((2 * piece_rows, queries), f32),
            shape((piece_rows, queries), f32),
            shape((pool_lines, slots), bf16),
            shape((slots, pool_lines), bf16),
            shape((n_head * CAP * LINES, slots), bf16),
            shape((2 * outs, n_head * CAP * LINES), bf16),
        ),
        pos,
        hit,
        asked,
        flops=3 * 10**9,
        traffic=3 * 10**6,
    )
    query, grad_out, bias = lax.optimization_barrier((query, grad_out, bias))
    twin_query = lax.ppermute(query, "head", twin)
    twin_grad = lax.ppermute(grad_out, "head", twin)
    lines_in = swap(lines_out, "ctx")
    mine = call(multiply, shape((pool_lines, line), bf16), send, lines_in)
    mine, twin_query, twin_grad = lax.optimization_barrier((mine, twin_query, twin_grad))
    from_below = lax.ppermute(mine, "head", up)
    from_above = lax.ppermute(mine, "head", down)
    onward = jnp.where(pos[1] & 1 == 0, from_below, from_above)
    from_far = lax.ppermute(onward, "head", relay)
    rows = queries * (grad_out.shape[1] // LAT)
    cols = 2 * rows

    def arrays(n):
        return shape((n * piece_rows, cols), f32), shape((n * piece_rows, cols), f32)

    row_stats = shape((8, cols), f32)
    scores, prob_grad, first_stats, keys, query_rows, grad_rows = call(
        score_own,
        (
            *arrays(1),
            row_stats,
            shape((piece_rows, width), bf16),
            shape((cols, width), bf16),
            shape((cols, LAT), bf16),
        ),
        mine,
        query,
        grad_out,
        twin_query,
        twin_grad,
        bias,
        flops=10**9,
        traffic=10**6,
        mib=14,
    )
    near_scores, near_prob_grad, near_stats, near_keys = call(
        score_near,
        (*arrays(2), row_stats, shape((2 * piece_rows, width), bf16)),
        from_below,
        from_above,
        query_rows,
        grad_rows,
        near_bias,
        scratch=(pltpu.VMEM((2 * piece_rows, queries), f32), pltpu.SemaphoreType.DMA(())),
        flops=2 * 10**9,
        traffic=10**6,
        mib=14,
        hbm=(4,),
    )
    far_scores, far_prob_grad, stats, tops, far_keys = call(
        score_far,
        (*arrays(1), row_stats, row_stats, shape((piece_rows, width), bf16)),
        from_far,
        query_rows,
        grad_rows,
        far_bias,
        first_stats,
        near_stats,
        scratch=(pltpu.VMEM((piece_rows, queries), f32), pltpu.SemaphoreType.DMA(())),
        flops=10**9,
        traffic=10**6,
        mib=14,
        hbm=(3,),
    )
    twin_stats = lax.ppermute(stats, "head", twin)

    def key_grad(first, n, dtype, e, d):
        return call(
            functools.partial(key_side, first=first),
            (shape((pool_lines, line), dtype),) * n + (shape((n * piece_rows, cols), bf16),),
            e,
            d,
            stats,
            twin_stats,
            tops,
            query_rows,
            grad_rows,
            flops=n * 10**9,
            traffic=10**6,
            mib=14,
        )

    to_far, far_score_grad = key_grad(3, 1, bf16, far_scores, far_prob_grad)
    sum_far = lax.ppermute(to_far, "head", across)
    to_down, to_up, near_score_grad = key_grad(1, 2, bf16, near_scores, near_prob_grad)
    sum_up = lax.ppermute(to_up, "head", up)
    sum_down = lax.ppermute(to_down, "head", down)
    to_own, score_grad = key_grad(0, 1, f32, scores, prob_grad)
    half_grad = shape((rows // 2, line), f32)
    query_mine, query_other = call(
        query_side,
        (half_grad, half_grad),
        score_grad,
        near_score_grad,
        far_score_grad,
        keys,
        near_keys,
        far_keys,
        flops=3 * 10**9,
        traffic=10**7,
    )
    query_got = lax.ppermute(query_other, "head", twin)
    query_grad = call(query_sum, shape(query.shape, bf16), query_mine, query_got)
    outbox = call(outgoing, shape((slots, line), bf16), back, to_own, sum_up, sum_down, sum_far)
    inbox = swap(outbox, "ctx")
    totals = call(multiply, shape((n_head * CAP * LINES, line), bf16), sums, inbox)
    spread = swap(totals, "head")
    grad_latent = call(place, shape((outs, width), f32), places, spread)
    return (query_grad, grad_latent)


def solution(mesh):
    return jax.shard_map(
        local,
        mesh=mesh,
        in_specs=(P("ctx", None), P("ctx", "head"), P("ctx", "head"), P("ctx", None)),
        out_specs=(P("ctx", "head"), P(("ctx", "head"), None)),
        check_vma=False,
    )
```

```python
import functools

import jax
import jax.numpy as jnp
from jax import lax
from jax.experimental import pallas as pl
from jax.experimental.pallas import tpu as pltpu
from jax.sharding import PartitionSpec as P

LAT = 512
BLOCK = 64
POOL = 36
CAP = 2
NEG = -1e30

score_scale = 192.0 ** (-0.5)
bf16 = jnp.bfloat16
f32 = jnp.float32


def iota(shape, dim):
    return lax.broadcasted_iota(jnp.int32, shape, dim)


def by20(x):
    return (x * 3277) >> 16


def dot(a, b, ca, cb):
    return lax.dot_general(a, b, (((ca,), (cb,)), ((), ())), preferred_element_type=f32)


def call(body, out_shape, *args, scratch=(), flops=0, traffic=0, mib=16, hbm=()):
    vmem = pl.BlockSpec(memory_space=pltpu.VMEM)
    smem = pl.BlockSpec(memory_space=pltpu.SMEM)
    specs = [smem if a.dtype == jnp.int32 and a.ndim == 1 else vmem for a in args]
    for i in hbm:
        specs[i] = pl.BlockSpec(memory_space=pl.ANY)
    return pl.pallas_call(
        body,
        out_shape=out_shape,
        in_specs=specs,
        out_specs=jax.tree.map(lambda _: vmem, out_shape),
        scratch_shapes=list(scratch),
        compiler_params=pltpu.CompilerParams(vmem_limit_bytes=mib * 1024 * 1024),
        cost_estimate=pl.CostEstimate(flops=flops, bytes_accessed=traffic, transcendentals=0),
    )(*args)


PART = 8
LINES = 4


def part_of(head):
    return head & 7


def near(head, step):
    return 2 * (((head >> 1) + step) & 3) + (head & 1)


def one_hot(mask):
    return jnp.where(mask, 1.0, 0.0).astype(bf16)


def own_part(pos_ref, lat_ref, out_ref):
    rows, tokens, width = out_ref.shape[0], lat_ref.shape[0], lat_ref.shape[1]
    row, col = iota((rows, tokens), 0), iota((rows, tokens), 1)
    want = (row >> 2) * BLOCK + part_of(pos_ref[1]) * PART + (row & 3)
    for u in (0, 1):
        lines = dot(one_hot(col == want + u * LINES), lat_ref[...], 1, 0)
        out_ref[:, u * width : (u + 1) * width] = lines.astype(bf16)


def hits(picks_ref, blocks):
    picks, queries = picks_ref.shape
    block = iota((blocks, queries), 0)
    least = jnp.full((blocks, queries), blocks, jnp.int32)
    for k in range(picks):
        least = jnp.minimum(least, picks_ref[k : k + 1, :] ^ block)
    return one_hot(least == 0)


def choose(picks_ref, ask_ref, *, per_owner):
    picks, queries = picks_ref.shape
    owners = ask_ref.shape[0]
    pick = picks_ref[...]
    owner = by20(pick)
    place = pick - owner * per_owner
    row = iota((owners, queries), 0)
    by_owner = [one_hot(owner[k : k + 1, :] == row) for k in range(picks)]
    by_place = [one_hot(place[k : k + 1, :] == row) for k in range(picks)]
    count = dot(jnp.concatenate(by_owner, axis=1), jnp.concatenate(by_place, axis=1), 1, 1)
    table = jnp.where(count > 0.5, 1.0, 0.0)
    before = one_hot(iota((owners, owners), 0) < iota((owners, owners), 1))
    rank = dot(table.astype(bf16), before, 1, 0)
    lane = iota((owners, owners), 1).astype(f32)
    ids = []
    for k in range(CAP):
        here = jnp.logical_and(table > 0.5, rank == k)
        ids.append(jnp.sum(jnp.where(here, lane, 0.0), axis=1, keepdims=True))
    line = iota(ask_ref.shape, 1)
    ask = jnp.where(line < LINES, ids[0][:, :, None], ids[1][:, :, None])
    ask_ref[...] = ask.astype(bf16)


def fetch(ask_ref, own_ref, out_ref):
    rows, lines = out_ref.shape[0], own_ref.shape[0]
    row, col = iota((rows, lines), 0), iota((rows, lines), 1)
    want = ask_ref[:, :1].astype(f32).astype(jnp.int32) * LINES + (row & 3)
    out_ref[...] = dot(one_hot(col == want), own_ref[...], 1, 0).astype(bf16)


def arrange(
    pos_ref, picks_ref, ask_ref, bias_ref, near_ref, far_ref, send_ref, back_ref, sum_ref, place_ref,
    *, first, per_dest, per_owner, blocks,
):
    queries = picks_ref.shape[1]
    hit = hits(picks_ref, blocks)
    rows, slots = send_ref.shape
    head = pos_ref[1]
    count = dot(jnp.ones((8, queries), bf16), hit, 1, 1)
    chosen8 = one_hot(count > 0.5)
    chosen = count[:1]
    lo, hi = iota((blocks, blocks), 0), iota((blocks, blocks), 1)
    order = dot(chosen8, one_hot(lo < hi), 1, 0)[:1]
    same = jnp.logical_and(lo < hi, lo >= by20(hi[:1]) * per_owner)
    rank = dot(chosen8, one_hot(same), 1, 0)[:1]
    row = iota((rows, blocks), 0)
    slot = (row >> 2).astype(f32)
    here = jnp.where(jnp.logical_and(order == slot, chosen > 0.5), 1.0, 0.0)
    block_id = jnp.sum(here * iota((rows, blocks), 1).astype(f32), axis=1, keepdims=True)
    block_rank = jnp.sum(here * rank, axis=1, keepdims=True)
    block_id = block_id.astype(jnp.int32)
    block_rank = block_rank.astype(jnp.int32)
    picked = dot(here.astype(bf16), hit, 1, 0)
    query_pos = first + pos_ref[0] * queries + iota((rows, queries), 1)
    base = block_id * BLOCK + (iota((rows, queries), 0) & 3) - query_pos
    for i, step in enumerate((0, -1, 1, 2)):
        out_ref = (bias_ref, near_ref, near_ref, far_ref)[i]
        for u in (0, 1):
            offset = near(head, step) * PART + u * LINES
            allowed = jnp.logical_and(picked > 0.5, base + offset <= 0)
            at = (2 * (i == 2) + u) * rows
            out_ref[at : at + rows, :] = jnp.where(allowed, 0.0, NEG)
    row = iota(send_ref.shape, 0)
    col = iota(send_ref.shape, 1)
    send = one_hot(col == (by20(block_id) * CAP + block_rank) * LINES + (row & 3))
    send_ref[...] = send
    unit = one_hot(iota((rows, rows), 0) == iota((rows, rows), 1))
    back_ref[...] = dot(send, unit, 0, 0).astype(bf16)
    ids = dot(one_hot(iota((8, 128), 1) == 0), ask_ref[...], 1, 1)[:1].astype(jnp.int32)
    row = iota(sum_ref.shape, 0)
    col = iota(sum_ref.shape, 1)
    e = part_of(head)
    dest = row >> 3
    start = ((per_dest * dest - e + 7) >> 3) + ((row >> 2) & 1)
    inside = 8 * start + e < per_dest * (dest + 1)
    match = jnp.logical_and(ids == start, (row & 3) == (col & 3))
    sum_ref[...] = one_hot(jnp.logical_and(match, inside))
    outs = place_ref.shape[0] // 2
    row = iota((outs, place_ref.shape[1]), 0)
    col = iota((outs, place_ref.shape[1]), 1)
    e = part_of(col >> 3)
    start = ((per_dest * head - e + 7) >> 3) + ((col >> 2) & 1)
    match = jnp.logical_and(8 * start + e == per_dest * head + (row >> 3), (row & 3) == (col & 3))
    for u in (0, 1):
        mine = jnp.logical_and(match, ((row >> 2) & 1) == u)
        place_ref[u * outs : (u + 1) * outs, :] = one_hot(mine)


def multiply(a_ref, b_ref, out_ref):
    out_ref[...] = dot(a_ref[...], b_ref[...], 1, 0).astype(out_ref.dtype)


def score_piece(keys, bias, qs_ref, gs_ref, e_ref, d_ref, at):
    tokens, cols = keys.shape[0], qs_ref.shape[0]
    wide = jnp.concatenate([bias] * (cols // bias.shape[1]), axis=1)
    s = dot(keys, qs_ref[...], 1, 1) * score_scale + wide
    d = dot(keys[:, :LAT], gs_ref[...], 1, 1)
    top = jnp.max(s, axis=0, keepdims=True)
    e = jnp.exp(s - top)
    e_ref[at : at + tokens, :] = e
    d_ref[at : at + tokens, :] = d
    return top, jnp.sum(e, axis=0, keepdims=True), jnp.sum(e * d, axis=0, keepdims=True)


def unpack(piece_ref, k_ref, at):
    lines, width = piece_ref.shape[0], k_ref.shape[1]
    for u in (0, 1):
        here = slice(at + u * lines, at + (u + 1) * lines)
        k_ref[here, :] = piece_ref[:, u * width : (u + 1) * width]


def score_own(
    own_ref, q_ref, g_ref, qt_ref, gt_ref, bias_ref, e_ref, d_ref, stat_ref, k_ref, qs_ref, gs_ref
):
    width = k_ref.shape[1]
    queries = q_ref.shape[0]
    heads = g_ref.shape[1] // LAT
    unpack(own_ref, k_ref, 0)
    for c, (x_ref, y_ref) in enumerate(((q_ref, g_ref), (qt_ref, gt_ref))):
        for h in range(heads):
            at = (c * heads + h) * queries
            qs_ref[at : at + queries, :] = x_ref[:, h * width : (h + 1) * width]
            gs_ref[at : at + queries, :] = y_ref[:, h * LAT : (h + 1) * LAT]
    found = score_piece(k_ref[...], bias_ref[...], qs_ref, gs_ref, e_ref, d_ref, 0)
    for i in range(3):
        stat_ref[i : i + 1, :] = found[i]
    stat_ref[3:8, :] = jnp.zeros((5, stat_ref.shape[1]), f32)


def score_near(
    below_ref, above_ref, qs_ref, gs_ref, bias_hbm, e_ref, d_ref, stat_ref, k_ref, bias_ref, sem
):
    copy = pltpu.make_async_copy(bias_hbm, bias_ref, sem)
    copy.start()
    size = 2 * below_ref.shape[0]
    unpack(below_ref, k_ref, 0)
    unpack(above_ref, k_ref, size)
    copy.wait()
    for i in (0, 1):
        at = slice(i * size, (i + 1) * size)
        found = score_piece(k_ref[at, :], bias_ref[at, :], qs_ref, gs_ref, e_ref, d_ref, i * size)
        for j in range(3):
            stat_ref[3 * i + j : 3 * i + j + 1, :] = found[j]
    stat_ref[6:8, :] = jnp.zeros((2, stat_ref.shape[1]), f32)


def score_far(
    far_ref, qs_ref, gs_ref, bias_hbm, own_ref, near_ref,
    e_ref, d_ref, stat_ref, tops_ref, k_ref, bias_ref, sem,
):
    copy = pltpu.make_async_copy(bias_hbm, bias_ref, sem)
    copy.start()
    unpack(far_ref, k_ref, 0)
    copy.wait()
    found = [tuple(own_ref[j : j + 1, :] for j in range(3))]
    for i in (0, 1):
        found.append(tuple(near_ref[3 * i + j : 3 * i + j + 1, :] for j in range(3)))
    found.append(score_piece(k_ref[...], bias_ref[...], qs_ref, gs_ref, e_ref, d_ref, 0))
    top = functools.reduce(jnp.maximum, [f[0] for f in found])
    weights = [jnp.exp(f[0] - top) for f in found]
    stat_ref[0:1, :] = top
    stat_ref[1:2, :] = sum(f[1] * w for f, w in zip(found, weights))
    stat_ref[2:3, :] = sum(f[2] * w for f, w in zip(found, weights))
    stat_ref[3:8, :] = jnp.zeros((5, stat_ref.shape[1]), f32)
    for i, f in enumerate(found):
        tops_ref[i : i + 1, :] = f[0]
    tops_ref[4:8, :] = jnp.zeros((4, stat_ref.shape[1]), f32)


def key_side(
    e_ref, d_ref, stat_ref, other_ref, tops_ref, qs_ref, gs_ref, *out_refs, first
):
    *outs, ds_ref = out_refs
    cols, width = qs_ref.shape
    mine = stat_ref[...]
    other = other_ref[...]
    other = jnp.concatenate([other[:, cols // 2 :], other[:, : cols // 2]], axis=1)
    top = jnp.maximum(mine[0:1], other[0:1])
    a, b = jnp.exp(mine[0:1] - top), jnp.exp(other[0:1] - top)
    inv = 1.0 / (mine[1:2] * a + other[1:2] * b)
    delta = (mine[2:3] * a + other[2:3] * b) * inv
    lines = outs[0].shape[0]
    size = 2 * lines
    for i, out_ref in enumerate(outs):
        at = slice(i * size, (i + 1) * size)
        scale = jnp.exp(tops_ref[first + i : first + i + 1, :] - top) * inv
        p = e_ref[at, :] * scale
        ds = (p * (d_ref[at, :] - delta)).astype(bf16)
        ds_ref[at, :] = ds
        dk = dot(ds, qs_ref[...], 1, 0) * score_scale
        dv = dot(p.astype(bf16), gs_ref[...], 1, 0)
        both = jnp.concatenate([dk[:, :LAT] + dv, dk[:, LAT:]], axis=1).astype(out_ref.dtype)
        for u in (0, 1):
            out_ref[:, u * width : (u + 1) * width] = both[u * lines : (u + 1) * lines, :]


def query_side(ds0_ref, ds1_ref, ds2_ref, k0_ref, k1_ref, k2_ref, mine_ref, other_ref):
    rows, width = mine_ref.shape[0], k0_ref.shape[1]
    for i, out_ref in enumerate((mine_ref, other_ref)):
        for u in (0, 1):
            at = slice((2 * i + u) * rows, (2 * i + u + 1) * rows)
            part = dot(ds0_ref[:, at], k0_ref[...], 0, 0)
            part = part + dot(ds1_ref[:, at], k1_ref[...], 0, 0)
            part = part + dot(ds2_ref[:, at], k2_ref[...], 0, 0)
            out_ref[:, u * width : (u + 1) * width] = part


def query_sum(mine_ref, got_ref, dq_ref):
    queries = dq_ref.shape[0]
    heads, line = mine_ref.shape[0] // queries, mine_ref.shape[1]
    width = line // 2
    for h in range(heads):
        at = slice(h * queries, (h + 1) * queries)
        total = ((mine_ref[at, :] + got_ref[at, :]) * score_scale).astype(bf16)
        dq_ref[:, h * width : (h + 1) * width] = total[:, :width]
        h2 = h + heads
        dq_ref[:, h2 * width : (h2 + 1) * width] = total[:, width:]


def outgoing(back_ref, own_ref, up_ref, down_ref, far_ref, out_ref):
    total = own_ref[...] + up_ref[...].astype(f32)
    total = total + down_ref[...].astype(f32) + far_ref[...].astype(f32)
    out_ref[...] = dot(back_ref[...], total.astype(bf16), 1, 0).astype(bf16)


def place(place_ref, in_ref, out_ref):
    outs, width = out_ref.shape
    first = dot(place_ref[:outs, :], in_ref[:, :width], 1, 0)
    out_ref[...] = first + dot(place_ref[outs:, :], in_ref[:, width:], 1, 0)


def local(latent, query, grad_out, picks):
    n_ctx = lax.axis_size("ctx")
    n_head = lax.axis_size("head")
    ctx_rows, width = latent.shape
    queries = query.shape[0]
    per_owner = ctx_rows // BLOCK
    blocks = per_owner * n_ctx
    line = 2 * width
    pool_lines = POOL * LINES
    slots = n_ctx * CAP * LINES
    piece_rows = 2 * pool_lines
    outs = ctx_rows // n_head
    pos = jnp.stack([lax.axis_index("ctx"), lax.axis_index("head")]).astype(jnp.int32)
    first = (ctx_rows - queries) * n_ctx
    shape = jax.ShapeDtypeStruct
    up = [(i, (i + 2) % n_head) for i in range(n_head)]
    down = [(i, (i - 2) % n_head) for i in range(n_head)]
    across = [(i, (i + 4 - 8 * (i & 1)) % n_head) for i in range(n_head)]
    relay = [(i, (i + 2 - 4 * (i & 1)) % n_head) for i in range(n_head)]
    twin = [(i, i ^ 1) for i in range(n_head)]

    def swap(x, axis):
        n = lax.axis_size(axis)
        x3 = x.reshape(n, -1, x.shape[1])
        return lax.all_to_all(x3, axis, split_axis=0, concat_axis=0, tiled=True).reshape(x.shape)

    picks = picks.T
    ask = call(
        functools.partial(choose, per_owner=per_owner),
        shape((n_ctx, CAP * LINES, 128), bf16),
        picks,
    )
    ask = ask.reshape(slots, 128)
    own = call(own_part, shape((per_owner * LINES, line), bf16), pos, latent, flops=10**9, traffic=10**6)
    asked = swap(ask, "ctx")
    lines_out = call(fetch, shape((slots, line), bf16), asked, own)
    bias, near_bias, far_bias, send, back, sums, places = call(
        functools.partial(arrange, first=first, per_dest=outs // PART, per_owner=per_owner, blocks=blocks),
        (
            shape((piece_rows, queries), f32),
            shape((2 * piece_rows, queries), f32),
            shape((piece_rows, queries), f32),
            shape((pool_lines, slots), bf16),
            shape((slots, pool_lines), bf16),
            shape((n_head * CAP * LINES, slots), bf16),
            shape((2 * outs, n_head * CAP * LINES), bf16),
        ),
        pos,
        picks,
        asked,
        flops=3 * 10**9,
        traffic=3 * 10**6,
    )
    query, grad_out, bias = lax.optimization_barrier((query, grad_out, bias))
    twin_query = lax.ppermute(query, "head", twin)
    twin_grad = lax.ppermute(grad_out, "head", twin)
    lines_in = swap(lines_out, "ctx")
    mine = call(multiply, shape((pool_lines, line), bf16), send, lines_in)
    mine, twin_query, twin_grad = lax.optimization_barrier((mine, twin_query, twin_grad))
    from_below = lax.ppermute(mine, "head", up)
    from_above = lax.ppermute(mine, "head", down)
    onward = jnp.where(pos[1] & 1 == 0, from_below, from_above)
    from_far = lax.ppermute(onward, "head", relay)
    rows = queries * (grad_out.shape[1] // LAT)
    cols = 2 * rows

    def arrays(n):
        return shape((n * piece_rows, cols), f32), shape((n * piece_rows, cols), f32)

    row_stats = shape((8, cols), f32)
    scores, prob_grad, first_stats, keys, query_rows, grad_rows = call(
        score_own,
        (
            *arrays(1),
            row_stats,
            shape((piece_rows, width), bf16),
            shape((cols, width), bf16),
            shape((cols, LAT), bf16),
        ),
        mine,
        query,
        grad_out,
        twin_query,
        twin_grad,
        bias,
        flops=10**9,
        traffic=10**6,
        mib=14,
    )
    near_scores, near_prob_grad, near_stats, near_keys = call(
        score_near,
        (*arrays(2), row_stats, shape((2 * piece_rows, width), bf16)),
        from_below,
        from_above,
        query_rows,
        grad_rows,
        near_bias,
        scratch=(pltpu.VMEM((2 * piece_rows, queries), f32), pltpu.SemaphoreType.DMA(())),
        flops=2 * 10**9,
        traffic=10**6,
        mib=14,
        hbm=(4,),
    )
    far_scores, far_prob_grad, stats, tops, far_keys = call(
        score_far,
        (*arrays(1), row_stats, row_stats, shape((piece_rows, width), bf16)),
        from_far,
        query_rows,
        grad_rows,
        far_bias,
        first_stats,
        near_stats,
        scratch=(pltpu.VMEM((piece_rows, queries), f32), pltpu.SemaphoreType.DMA(())),
        flops=10**9,
        traffic=10**6,
        mib=14,
        hbm=(3,),
    )
    twin_stats = lax.ppermute(stats, "head", twin)

    def key_grad(first, n, dtype, e, d):
        return call(
            functools.partial(key_side, first=first),
            (shape((pool_lines, line), dtype),) * n + (shape((n * piece_rows, cols), bf16),),
            e,
            d,
            stats,
            twin_stats,
            tops,
            query_rows,
            grad_rows,
            flops=n * 10**9,
            traffic=10**6,
            mib=14,
        )

    to_far, far_score_grad = key_grad(3, 1, bf16, far_scores, far_prob_grad)
    sum_far = lax.ppermute(to_far, "head", across)
    to_down, to_up, near_score_grad = key_grad(1, 2, bf16, near_scores, near_prob_grad)
    sum_up = lax.ppermute(to_up, "head", up)
    sum_down = lax.ppermute(to_down, "head", down)
    to_own, score_grad = key_grad(0, 1, f32, scores, prob_grad)
    half_grad = shape((rows // 2, line), f32)
    query_mine, query_other = call(
        query_side,
        (half_grad, half_grad),
        score_grad,
        near_score_grad,
        far_score_grad,
        keys,
        near_keys,
        far_keys,
        flops=3 * 10**9,
        traffic=10**7,
    )
    query_got = lax.ppermute(query_other, "head", twin)
    query_grad = call(query_sum, shape(query.shape, bf16), query_mine, query_got)
    outbox = call(outgoing, shape((slots, line), bf16), back, to_own, sum_up, sum_down, sum_far)
    inbox = swap(outbox, "ctx")
    totals = call(multiply, shape((n_head * CAP * LINES, line), bf16), sums, inbox)
    spread = swap(totals, "head")
    grad_latent = call(place, shape((outs, width), f32), places, spread)
    return (query_grad, grad_latent)


def solution(mesh):
    return jax.shard_map(
        local,
        mesh=mesh,
        in_specs=(P("ctx", None), P("ctx", "head"), P("ctx", "head"), P("ctx", None)),
        out_specs=(P("ctx", "head"), P(("ctx", "head"), None)),
        check_vma=False,
    )
```
